32 devices in a mesh: fsdp: 4 (over z), ctx: 2 (over core), tp: 4 (over y, x).
Axes of the slice: x: 2, y: 2, z: 4, core: 2. Of those that a mesh axis runs over, the one named last changes fastest.
Arguments:
- block_input: bfloat16 [4, 2048, 2048], P('fsdp', 'ctx'), may hold values from -6 to 6
- segment_ids: int32 [4, 2048], P('fsdp', 'ctx'), may hold values from 0 to 15, never falling along the last dimension, each value on 1 to 1024 neighbouring positions
- positions: int32 [4, 2048], P('fsdp', 'ctx'), may hold values from 0 to 8191
- out_cotangent: bfloat16 [4, 2048, 2048], P('fsdp', 'ctx'), may hold values from -6 to 6
- norm_gains: float32 [2, 2048], P(None, ('fsdp', 'ctx')), may hold values from 0.5 to 1.5
- qkv_weight: float32 [3, 2048, 2048], P(None, ('fsdp', 'ctx'), 'tp'), may hold values from -0.125 to 0.125
- outproj_weight: float32 [2048, 2048], P(('fsdp', 'ctx'), 'tp'), may hold values from -1 to 1
- gateup_weight: float32 [2, 2048, 8192], P(None, ('fsdp', 'ctx'), 'tp'), may hold values from -0.125 to 0.125
- down_weight: float32 [2048, 8192], P(('fsdp', 'ctx'), 'tp'), may hold values from -0.0625 to 0.0625
- moment_norm: float32 [2, 2048], P(None, ('fsdp', 'ctx')), may hold values from -256 to 256
- moment_qkv: float32 [3, 2048, 2048], P(None, ('fsdp', 'ctx'), 'tp'), may hold values from -112 to 112
- moment_outproj: float32 [2048, 2048], P(('fsdp', 'ctx'), 'tp'), may hold values from -40 to 40
- moment_gateup: float32 [2, 2048, 8192], P(None, ('fsdp', 'ctx'), 'tp'), may hold values from -40 to 40
- moment_down: float32 [2048, 8192], P(('fsdp', 'ctx'), 'tp'), may hold values from -80 to 80
- square_norm: float32 [2, 2048], P(None, ('fsdp', 'ctx')), may hold values from 512 to 5120
- square_qkv: float32 [3, 2048, 2048], P(None, ('fsdp', 'ctx'), 'tp'), may hold values from 81.92 to 819.2
- square_outproj: float32 [2048, 2048], P(('fsdp', 'ctx'), 'tp'), may hold values from 13.1072 to 131.072
- square_gateup: float32 [2, 2048, 8192], P(None, ('fsdp', 'ctx'), 'tp'), may hold values from 13.1072 to 131.072
- square_down: float32 [2048, 8192], P(('fsdp', 'ctx'), 'tp'), may hold values from 52.4288 to 524.288
Outputs:
- block_out: bfloat16 [4, 2048, 2048], P('fsdp', 'ctx')
- input_grad: bfloat16 [4, 2048, 2048], P('fsdp', 'ctx')
- norm_grad: float32 [2, 2048], P(None, ('fsdp', 'ctx'))
- qkv_grad: float32 [3, 2048, 2048], P(None, ('fsdp', 'ctx'), 'tp')
- outproj_grad: float32 [2048, 2048], P(('fsdp', 'ctx'), 'tp')
- gateup_grad: float32 [2, 2048, 8192], P(None, ('fsdp', 'ctx'), 'tp')
- down_grad: float32 [2048, 8192], P(('fsdp', 'ctx'), 'tp')
- new_norm: float32 [2, 2048], P(None, ('fsdp', 'ctx'))
- new_qkv: float32 [3, 2048, 2048], P(None, ('fsdp', 'ctx'), 'tp')
- new_outproj: float32 [2048, 2048], P(('fsdp', 'ctx'), 'tp')
- new_gateup: float32 [2, 2048, 8192], P(None, ('fsdp', 'ctx'), 'tp')
- new_down: float32 [2048, 8192], P(('fsdp', 'ctx'), 'tp')
- new_moment_norm: float32 [2, 2048], P(None, ('fsdp', 'ctx'))
- new_moment_qkv: float32 [3, 2048, 2048], P(None, ('fsdp', 'ctx'), 'tp')
- new_moment_outproj: float32 [2048, 2048], P(('fsdp', 'ctx'), 'tp')
- new_moment_gateup: float32 [2, 2048, 8192], P(None, ('fsdp', 'ctx'), 'tp')
- new_moment_down: float32 [2048, 8192], P(('fsdp', 'ctx'), 'tp')
- new_square_norm: float32 [2, 2048], P(None, ('fsdp', 'ctx'))
- new_square_qkv: float32 [3, 2048, 2048], P(None, ('fsdp', 'ctx'), 'tp')
- new_square_outproj: float32 [2048, 2048], P(('fsdp', 'ctx'), 'tp')
- new_square_gateup: float32 [2, 2048, 8192], P(None, ('fsdp', 'ctx'), 'tp')
- new_square_down: float32 [2048, 8192], P(('fsdp', 'ctx'), 'tp')
The draws below stay inside these ranges and needn't reach their ends.
Inputs may be any that keep to these rules, and one draw needn't show every extreme that they name: `segment_ids`: within a sequence ids start at 0 and never fall; a document holds at most 1024 tokens and some document holds exactly that many.
All inputs are finite; a program needn't handle non-finite values.
Results may differ from the reference program's by a relative error of at most 0.017.
The reference program's roundings to bfloat16 on the way count: a program that leaves them out, or rounds other values in their place, can miss the bound.
Values may be sent and summed in bfloat16 or wider, within the bound.
No kernel may reach another device: no remote copies, remote signals or barrier semaphores. Data moves between devices by JAX's collectives and lax.ppermute only.
A program may use at most 448 MiB of HBM per device.

```python
import math
import jax
import jax.numpy as jnp
import numpy as np
from jax import lax

D = 2048
HEADS = 32
HEAD_DIM = 64
FF = 8192
LEN = 2048
STEP = 10
SEQS = 4


def set_ends(entries, key, least, high):
    shape = entries.shape
    spot = [jax.random.randint(jax.random.fold_in(key, axis), (), 0, shape[axis]) for axis in range(len(shape))]
    entries = entries.at[tuple(spot)].set(least)
    longest = shape.index(max(shape))
    spot[longest] = (spot[longest] + 1) % shape[longest]
    return entries.at[tuple(spot)].set(high)


def block_levels(key, dims, cuts, low, largest):
    level, own = 1.0, jax.random.fold_in(key, 6)
    for position, parts in cuts:
        heights = jnp.exp(jax.random.uniform(jax.random.fold_in(own, position), (parts,), jnp.float32, low / len(cuts), largest / len(cuts)))
        level = level * jnp.repeat(heights, dims[position] // parts).reshape([-1 if axis == position else 1 for axis in range(len(dims))])
    return level


def profile(amount, total, bound, lean):
    weights = [(1 << 20) // math.isqrt(standing ** lean) + 1 for standing in range(2, amount + 1)]
    spare, holding = total - bound - (amount - 1), [1] * (amount - 1)
    while spare > 0:
        free = [i for i in range(amount - 1) if holding[i] < bound]
        whole, left = sum([weights[i] for i in free]), spare
        for i in free:
            extra = min(bound - holding[i], max(1, left * weights[i] // whole), spare)
            holding[i] = holding[i] + extra
            spare = spare - extra
    return np.array([bound] + holding)


def uneven_parts(stream_key, amount, total, limit, skew):
    if amount == 2:
        one = jax.random.randint(stream_key, (), max(1, total - limit), min(limit, total - 1) + 1)
        return jnp.stack([one, total - one])
    sizes = jnp.asarray(profile(amount, total, limit, skew), jnp.int32)
    couples = (amount - 1) // 2
    source_of, sink = sizes[1:1 + 2 * couples:2], sizes[2:2 + 2 * couples:2]
    room = jnp.minimum(source_of - 1, limit - sink)
    passed = jax.random.randint(jax.random.fold_in(stream_key, 1), (couples,), 0, 1 << 20) % (room + 1)
    sizes = sizes.at[1:1 + 2 * couples:2].set(source_of - passed).at[2:2 + 2 * couples:2].set(sink + passed)
    return sizes[jax.random.permutation(jax.random.fold_in(stream_key, 2), amount)]


def normal_values(rng, shape, spread, bound, shards=(), held_as=jnp.bfloat16):
    array = spread * jax.random.normal(rng, shape, jnp.float32)
    if shards:
        array = array * block_levels(rng, shape, shards, -0.22, 0.18)
    return jnp.clip(array, -bound, bound).astype(held_as)


def setup_inputs(seed: int = 0) -> dict:
    streams_of = jax.random.split(jax.random.key(seed), 20)
    return {
        "block_input": normal_values(streams_of[0], (SEQS, LEN, D), 1.0, 6.0, ((0, 4), (1, 2))),
        "segment_ids": jax.vmap(lambda own: jnp.searchsorted(jnp.cumsum(uneven_parts(own, max(4, LEN // 128), LEN, LEN // 2, 1)), jnp.arange(LEN), side="right"))(jax.random.split(streams_of[1], SEQS)).reshape((SEQS, LEN)).astype(jnp.int32),
        "positions": set_ends(jax.random.randint(streams_of[2], (SEQS, LEN), 0, 4 * LEN), jax.random.fold_in(streams_of[2], 1), 0, (4 * LEN) - 1).astype(jnp.int32),
        "out_cotangent": normal_values(streams_of[3], (SEQS, LEN, D), 1.0, 6.0, ((0, 4), (1, 2))),
        "norm_gains": jnp.clip(1.0 + 0.1 * jax.random.normal(streams_of[4], (2, D), jnp.float32), 0.5, 1.5),
        "qkv_weight": normal_values(streams_of[5], (3, D, D), D ** -0.5, 0.125, ((1, 8), (2, 4)), jnp.float32),
        "outproj_weight": normal_values(streams_of[6], (D, D), (D // 64) ** -0.5, 1.0, ((0, 8), (1, 4)), jnp.float32),
        "gateup_weight": normal_values(streams_of[7], (2, D, FF), D ** -0.5, 0.125, ((1, 8), (2, 4)), jnp.float32),
        "down_weight": normal_values(streams_of[8], (D, FF), FF ** -0.5, 0.0625, ((0, 8), (1, 4)), jnp.float32),
        "moment_norm": normal_values(streams_of[9], (2, D), (0.5 * (SEQS * LEN) ** 0.5), 256.0, ((1, 8),), jnp.float32),
        "moment_qkv": normal_values(streams_of[10], (3, D, D), (0.2 * (SEQS * LEN) ** 0.5), 112.0, ((1, 8), (2, 4)), jnp.float32),
        "moment_outproj": normal_values(streams_of[11], (D, D), (0.08 * (SEQS * LEN) ** 0.5), 40.0, ((0, 8), (1, 4)), jnp.float32),
        "moment_gateup": normal_values(streams_of[12], (2, D, FF), (0.08 * (SEQS * LEN) ** 0.5), 40.0, ((1, 8), (2, 4)), jnp.float32),
        "moment_down": normal_values(streams_of[13], (D, FF), (0.16 * (SEQS * LEN) ** 0.5), 80.0, ((0, 8), (1, 4)), jnp.float32),
        "square_norm": jnp.clip(jnp.exp(math.log(5120.0) - 2.3025851 * jax.random.uniform(streams_of[14], (2, D), jnp.float32) ** block_levels(streams_of[14], (2, D), ((1, 8),), -0.2, 0.2)), 512.0, 5120.0),
        "square_qkv": jnp.clip(jnp.exp(math.log(819.2) - 2.3025851 * jax.random.uniform(streams_of[15], (3, D, D), jnp.float32) ** block_levels(streams_of[15], (3, D, D), ((1, 8), (2, 4)), -0.2, 0.2)), 81.92, 819.2),
        "square_outproj": jnp.clip(jnp.exp(math.log(131.072) - 2.3025852 * jax.random.uniform(streams_of[16], (D, D), jnp.float32) ** block_levels(streams_of[16], (D, D), ((0, 8), (1, 4)), -0.2, 0.2)), 13.1072, 131.072),
        "square_gateup": jnp.clip(jnp.exp(math.log(131.072) - 2.3025852 * jax.random.uniform(streams_of[17], (2, D, FF), jnp.float32) ** block_levels(streams_of[17], (2, D, FF), ((1, 8), (2, 4)), -0.2, 0.2)), 13.1072, 131.072),
        "square_down": jnp.clip(jnp.exp(math.log(524.288) - 2.3025852 * jax.random.uniform(streams_of[18], (D, FF), jnp.float32) ** block_levels(streams_of[18], (D, FF), ((0, 8), (1, 4)), -0.2, 0.2)), 52.4288, 524.288),
    }


beta_one = 0.9
beta_two = 0.95
adam_eps = 1e-08
decay_rate = 0.1

def rope_tables(where_at):
    half = HEAD_DIM // 2
    freqs = jnp.exp(jnp.arange(half, dtype=jnp.float32) * (-2.0 * math.log(130000.0) / HEAD_DIM))
    angles = where_at.astype(jnp.float32)[..., None] * freqs
    return (jnp.cos(angles), jnp.sin(angles))

def rotate(tensor, cosine, sine):
    half = tensor.shape[-1] // 2
    first = tensor[..., :half]
    second = tensor[..., half:]
    cosine = cosine[..., None, :]
    sine = sine[..., None, :]
    return jnp.concatenate([first * cosine - second * sine, second * cosine + first * sine], -1)

def normalize(values):
    scale = lax.rsqrt(lax.optimization_barrier(jnp.mean(values * values, -1, keepdims=True)) + 1e-05)
    return (values * scale, scale)

def norm_back(upstream, normed, scale, weights):
    scaled = upstream * weights
    return (scale * (scaled - normed * lax.optimization_barrier(jnp.mean(scaled * normed, -1, keepdims=True))), lax.optimization_barrier(jnp.sum(upstream * normed, 0)))

def adamw(weight, gradient, moment, square, step_size):
    moment_new = beta_one * moment + (1.0 - beta_one) * gradient
    square_new = beta_two * square + (1.0 - beta_two) * gradient * gradient
    moment_hat = moment_new / (1.0 - beta_one ** STEP)
    square_hat = square_new / (1.0 - beta_two ** STEP)
    weight_new = weight - step_size * (moment_hat / (jnp.sqrt(square_hat) + adam_eps) + decay_rate * weight)
    return (weight_new, moment_new, square_new)

def reference(block_input, segment_ids, positions, out_cotangent, norm_gains, qkv_weight, outproj_weight, gateup_weight, down_weight, moment_norm, moment_qkv, moment_outproj, moment_gateup, moment_down, square_norm, square_qkv, square_outproj, square_gateup, square_down):
    bf16 = jnp.bfloat16
    f32 = jnp.float32
    gains16 = norm_gains.astype(bf16)
    gain_attn = gains16[0].astype(f32)
    gain_mlp = gains16[1].astype(f32)
    qkv16 = qkv_weight.astype(bf16)
    qkv32 = qkv16.astype(f32)
    outproj16 = outproj_weight.astype(bf16)
    gateup16 = gateup_weight.astype(bf16)
    down16 = down_weight.astype(bf16)

    def one_sequence(carry, inputs):
        tokens16, segs, where_at, cotan16 = inputs
        length = tokens16.shape[0]
        inputs32 = tokens16.astype(f32)
        normed_one, scale_one = normalize(inputs32)
        act_one = (normed_one * gain_attn).astype(bf16)
        projected = jnp.einsum('nd,jdc->jnc', act_one.astype(f32), qkv32)
        cosine, sine = rope_tables(where_at)
        head_shape = (length, HEADS, HEAD_DIM)
        query16 = rotate(projected[0].reshape(head_shape), cosine, sine).astype(bf16)
        key16 = rotate(projected[1].reshape(head_shape), cosine, sine).astype(bf16)
        value16 = projected[2].reshape(head_shape).astype(bf16)
        index = jnp.arange(length)
        allowed = (index[None, :] <= index[:, None]) & (segs[None, :] == segs[:, None])
        scores = jnp.einsum('qhe,khe->hqk', query16.astype(f32), key16.astype(f32)) * 0.125
        scores = jnp.where(allowed[None], scores, -jnp.inf)
        top = lax.optimization_barrier(jnp.max(scores, -1, keepdims=True))
        log_total = top + jnp.log(lax.optimization_barrier(jnp.sum(jnp.exp(scores - top), -1, keepdims=True)))
        probs = jnp.exp(scores - log_total)
        probs16 = probs.astype(bf16)
        attended16 = jnp.einsum('hqk,khe->qhe', probs16.astype(f32), value16.astype(f32)).astype(bf16).reshape(length, D)
        resid = inputs32 + jnp.dot(attended16, outproj16.T, preferred_element_type=f32)
        normed_two, scale_two = normalize(resid)
        act_two = (normed_two * gain_mlp).astype(bf16)
        gate_pre = jnp.dot(act_two, gateup16[0], preferred_element_type=f32)
        up_pre = jnp.dot(act_two, gateup16[1], preferred_element_type=f32)
        sigma = jax.nn.sigmoid(gate_pre)
        inner16 = (gate_pre * sigma * up_pre).astype(bf16)
        output16 = (resid + jnp.dot(inner16, down16.T, preferred_element_type=f32)).astype(bf16)
        cotan32 = cotan16.astype(f32)
        dinner = jnp.dot(cotan16, down16, preferred_element_type=f32)
        down_part = jnp.dot(cotan16.T, inner16, preferred_element_type=f32)
        dgate16 = (dinner * up_pre * sigma * (1.0 + gate_pre * (1.0 - sigma))).astype(bf16)
        dup16 = (dinner * gate_pre * sigma).astype(bf16)
        gate_part = jnp.dot(act_two.T, dgate16, preferred_element_type=f32)
        up_part = jnp.dot(act_two.T, dup16, preferred_element_type=f32)
        dact_two = jnp.dot(dgate16, gateup16[0].T, preferred_element_type=f32) + jnp.dot(dup16, gateup16[1].T, preferred_element_type=f32)
        dnorm_two, gain_two_part = norm_back(dact_two, normed_two, scale_two, gain_mlp)
        dresid = cotan32 + dnorm_two
        dresid16 = dresid.astype(bf16)
        outproj_part = jnp.dot(dresid16.T, attended16, preferred_element_type=f32)
        dattended16 = jnp.dot(dresid16, outproj16, preferred_element_type=f32).astype(bf16)
        dattended3 = dattended16.reshape(head_shape).astype(f32)
        dprobs = jnp.einsum('qhe,khe->hqk', dattended3, value16.astype(f32))
        delta = jnp.einsum('qhe,qhe->hq', dattended3, attended16.reshape(head_shape).astype(f32))[..., None]
        dscores16 = (probs * (dprobs - delta)).astype(bf16)
        dquery = 0.125 * jnp.einsum('hqk,khe->qhe', dscores16.astype(f32), key16.astype(f32))
        dkey = 0.125 * jnp.einsum('hqk,qhe->khe', dscores16.astype(f32), query16.astype(f32))
        dvalue = jnp.einsum('hqk,qhe->khe', probs16.astype(f32), dattended3)
        dquery16 = rotate(dquery, cosine, -sine).astype(bf16).reshape(length, D)
        dkey16 = rotate(dkey, cosine, -sine).astype(bf16).reshape(length, D)
        dvalue16 = dvalue.astype(bf16).reshape(length, D)
        dproj = jnp.stack([dquery16, dkey16, dvalue16]).astype(f32)
        qkv_part = jnp.einsum('nd,jnc->jdc', act_one.astype(f32), dproj)
        dact_one = jnp.einsum('jnc,jdc->nd', dproj, qkv32)
        dnorm_one, gain_one_part = norm_back(dact_one, normed_one, scale_one, gain_attn)
        dinput16 = (dresid + dnorm_one).astype(bf16)
        gains_acc, qkv_acc, outproj_acc, gateup_acc, down_acc = carry
        carry = (gains_acc + jnp.stack([gain_one_part, gain_two_part]), qkv_acc + qkv_part, outproj_acc + outproj_part, gateup_acc + jnp.stack([gate_part, up_part]), down_acc + down_part)
        return (carry, (output16, dinput16))
    start = (jnp.zeros((2, D), f32), jnp.zeros((3, D, D), f32), jnp.zeros((D, D), f32), jnp.zeros((2, D, FF), f32), jnp.zeros((D, FF), f32))
    grads, (block_out, input_grad) = lax.scan(one_sequence, start, (block_input, segment_ids, positions, out_cotangent))
    norm_grad, qkv_grad, outproj_grad, gateup_grad, down_grad = grads
    new_norm, new_moment_norm, new_square_norm = adamw(norm_gains, norm_grad, moment_norm, square_norm, 0.4)
    new_qkv, new_moment_qkv, new_square_qkv = adamw(qkv_weight, qkv_grad, moment_qkv, square_qkv, 0.4 / math.sqrt(D))
    new_outproj, new_moment_outproj, new_square_outproj = adamw(outproj_weight, outproj_grad, moment_outproj, square_outproj, 0.4 / math.sqrt(D // 64))
    new_gateup, new_moment_gateup, new_square_gateup = adamw(gateup_weight, gateup_grad, moment_gateup, square_gateup, 0.4 / math.sqrt(D))
    new_down, new_moment_down, new_square_down = adamw(down_weight, down_grad, moment_down, square_down, 0.4 / math.sqrt(FF))
    return (block_out, input_grad, norm_grad, qkv_grad, outproj_grad, gateup_grad, down_grad, new_norm, new_qkv, new_outproj, new_gateup, new_down, new_moment_norm, new_moment_qkv, new_moment_outproj, new_moment_gateup, new_moment_down, new_square_norm, new_square_qkv, new_square_outproj, new_square_gateup, new_square_down)
```

```python
import functools
import math

import jax
import jax.numpy as jnp
from jax import lax
from jax.experimental import pallas as pl
from jax.experimental.pallas import tpu as pltpu
from jax.sharding import PartitionSpec as P

D = 2048
HEAD_DIM = 64
FF = 8192
STEP = 10

bf16 = jnp.bfloat16
f32 = jnp.float32

beta_one = 0.9
beta_two = 0.95
adam_eps = 1e-08
decay_rate = 0.1

BLOCK = 256
PAIR = 2 * HEAD_DIM
HIDDEN = -1e30
VMEM = 56 * 1024 * 1024


def rope_tables(where_at):
    half = HEAD_DIM // 2
    freqs = jnp.exp(jnp.arange(half, dtype=f32) * (-2.0 * math.log(130000.0) / HEAD_DIM))
    angles = where_at.astype(f32)[..., None] * freqs
    cosine, sine = jnp.cos(angles), jnp.sin(angles)
    return (
        jnp.concatenate([cosine, cosine, cosine, cosine], -1),
        jnp.concatenate([-sine, sine, -sine, sine], -1),
    )


def turn(values, cosine, sine):
    columns = values.shape[1]
    lane = lax.broadcasted_iota(jnp.int32, (values.shape[0], PAIR), 1)
    low = (lane % HEAD_DIM) < HEAD_DIM // 2
    parts = []
    for at in range(0, columns, PAIR):
        tile = values[:, at : at + PAIR]
        other = jnp.where(
            low,
            pltpu.roll(tile, PAIR - HEAD_DIM // 2, 1),
            pltpu.roll(tile, HEAD_DIM // 2, 1),
        )
        parts.append(tile * cosine + other * sine)
    return parts


def normalize(values):
    scale = lax.rsqrt(jnp.mean(values * values, -1, keepdims=True) + 1e-05)
    return (values * scale, scale)


def norm_back(upstream, normed, scale, weights):
    scaled = upstream * weights
    return (
        scale * (scaled - normed * jnp.mean(scaled * normed, -1, keepdims=True)),
        jnp.sum(upstream * normed, 0),
    )


def dot(one, two, dims=((1,), (0,))):
    return lax.dot_general(one, two, (dims, ((), ())), preferred_element_type=f32)


ROWS = ((1,), (1,))
OVER = ((0,), (0,))


def project_kernel(x_ref, w_ref, cos_ref, sin_ref, out_ref):
    columns = out_ref.shape[1] // 3
    x = x_ref[...]
    for j in range(3):
        made = dot(x, w_ref[:, j * columns : (j + 1) * columns])
        if j < 2:
            for at, part in enumerate(turn(made, cos_ref[...], sin_ref[...])):
                start = j * columns + at * PAIR
                out_ref[:, start : start + PAIR] = part.astype(bf16)
        else:
            out_ref[:, j * columns :] = made.astype(bf16)


def project(act, weight, cosine, sine):
    rows, width = act.shape
    columns = weight.shape[1]
    return pl.pallas_call(
        project_kernel,
        grid=(rows // BLOCK,),
        in_specs=[
            pl.BlockSpec((BLOCK, width), lambda i: (i, 0)),
            pl.BlockSpec((width, columns), lambda i: (0, 0)),
            pl.BlockSpec((BLOCK, PAIR), lambda i: (i, 0)),
            pl.BlockSpec((BLOCK, PAIR), lambda i: (i, 0)),
        ],
        out_specs=pl.BlockSpec((BLOCK, columns), lambda i: (i, 0)),
        out_shape=jax.ShapeDtypeStruct((rows, columns), bf16),
        compiler_params=pltpu.CompilerParams(vmem_limit_bytes=VMEM),
        cost_estimate=pl.CostEstimate(
            flops=2 * rows * width * columns,
            bytes_accessed=2 * (rows * width + width * columns + rows * columns),
            transcendentals=0,
        ),
        name="project_rope",
    )(act, weight, cosine, sine)


def head_halves(pair):
    first = lax.broadcasted_iota(jnp.int32, pair.shape, 1) < HEAD_DIM
    zero = jnp.zeros_like(pair)
    return jnp.where(first, pair, zero), jnp.where(first, zero, pair)


def masked(scores, seg_k, seg_q, offset):
    key = lax.broadcasted_iota(jnp.int32, scores.shape, 0)
    query = lax.broadcasted_iota(jnp.int32, scores.shape, 1)
    seen = (key - query <= offset) & (seg_k == seg_q)
    return jnp.where(seen, scores, HIDDEN)


def attend_kernel(
    blocks_before, low_ref, q_ref, kv_ref, seg_k_ref, seg_q_ref, out_ref, lse_ref, scores, v_turned
):
    i = pl.program_id(0)
    columns = q_ref.shape[1]
    low = low_ref[i]
    high = blocks_before + i + 1

    @pl.when(i == 0)
    def _():
        for at in range(0, columns, PAIR):
            v_turned[at : at + PAIR, :] = kv_ref[:, columns + at : columns + at + PAIR].T

    seg_q = seg_q_ref[...]
    for pair in range(columns // PAIR):
        at = pair * PAIR
        queries = head_halves(q_ref[:, at : at + PAIR])

        def score(j, tops):
            rows = pl.ds(pl.multiple_of(j * BLOCK, BLOCK), BLOCK)
            keys = kv_ref[rows, at : at + PAIR]
            seg_k = seg_k_ref[rows, :]
            new = []
            for h in range(2):
                raw = dot(keys, queries[h], ROWS) * 0.125
                raw = masked(raw, seg_k, seg_q, (blocks_before + i - j) * BLOCK)
                scores[h, rows, :] = raw
                new.append(jnp.maximum(tops[h], jnp.max(raw, 0, keepdims=True)))
            return tuple(new)

        start = jnp.full((1, BLOCK), HIDDEN, f32)
        tops = lax.fori_loop(low, high, score, (start, start))

        def weigh(j, totals):
            rows = pl.ds(pl.multiple_of(j * BLOCK, BLOCK), BLOCK)
            new = []
            for h in range(2):
                power = jnp.exp(scores[h, rows, :] - tops[h])
                scores[h, rows, :] = power
                new.append(totals[h] + jnp.sum(power, 0, keepdims=True))
            return tuple(new)

        start = jnp.zeros((1, BLOCK), f32)
        totals = lax.fori_loop(low, high, weigh, (start, start))
        shares = tuple(1.0 / total for total in totals)

        def mix(j, sums):
            rows = pl.ds(pl.multiple_of(j * BLOCK, BLOCK), BLOCK)
            new = []
            for h in range(2):
                probs = (scores[h, rows, :] * shares[h]).astype(bf16)
                values = v_turned[at + h * HEAD_DIM : at + (h + 1) * HEAD_DIM, rows]
                new.append(sums[h] + dot(values, probs))
            return tuple(new)

        start = jnp.zeros((HEAD_DIM, BLOCK), f32)
        sums = lax.fori_loop(low, high, mix, (start, start))
        out_ref[:, at : at + PAIR] = jnp.concatenate(sums, 0).T.astype(bf16)
        for h in range(2):
            lse_ref[2 * pair + h : 2 * pair + h + 1, :] = tops[h] + jnp.log(totals[h])


def attend(low, query, kv_all, seg_col, seg_row):
    rows, columns = query.shape
    keys = kv_all.shape[0]
    heads = columns // HEAD_DIM
    whole = lambda i, low: (0, 0)
    return pl.pallas_call(
        functools.partial(attend_kernel, (keys - rows) // BLOCK),
        grid_spec=pltpu.PrefetchScalarGridSpec(
            num_scalar_prefetch=1,
            grid=(rows // BLOCK,),
            in_specs=[
                pl.BlockSpec((BLOCK, columns), lambda i, low: (i, 0)),
                pl.BlockSpec((keys, 2 * columns), whole),
                pl.BlockSpec((keys, 1), whole),
                pl.BlockSpec((1, BLOCK), lambda i, low: (0, i)),
            ],
            out_specs=[
                pl.BlockSpec((BLOCK, columns), lambda i, low: (i, 0)),
                pl.BlockSpec((heads, BLOCK), lambda i, low: (0, i)),
            ],
            scratch_shapes=[
                pltpu.VMEM((2, keys, BLOCK), f32),
                pltpu.VMEM((columns, keys), bf16),
            ],
        ),
        out_shape=[
            jax.ShapeDtypeStruct((rows, columns), bf16),
            jax.ShapeDtypeStruct((heads, rows), f32),
        ],
        compiler_params=pltpu.CompilerParams(vmem_limit_bytes=VMEM),
        cost_estimate=pl.CostEstimate(
            flops=2 * rows * keys * columns,
            bytes_accessed=2 * (2 * rows * columns + 2 * keys * columns),
            transcendentals=rows * keys * heads // 4,
        ),
        name="attend",
    )(low, query, kv_all, seg_col, seg_row)


def attend_back_kernel(
    blocks_before,
    low_ref,
    q_ref,
    kv_ref,
    seg_k_ref,
    seg_q_ref,
    lse_ref,
    att_ref,
    datt_ref,
    cos_ref,
    sin_ref,
    dq_ref,
    dkv_ref,
    k_turned,
):
    i = pl.program_id(0)
    columns = q_ref.shape[1]
    low = low_ref[i]
    high = blocks_before + i + 1

    @pl.when(i == 0)
    def _():
        dkv_ref[...] = jnp.zeros_like(dkv_ref)
        for at in range(0, columns, PAIR):
            k_turned[at : at + PAIR, :] = kv_ref[:, at : at + PAIR].T

    seg_q = seg_q_ref[...]
    for pair in range(columns // PAIR):
        at = pair * PAIR
        queries = head_halves(q_ref[:, at : at + PAIR])
        upstream16 = datt_ref[:, at : at + PAIR]
        upstream = head_halves(upstream16)
        both = (upstream16.astype(f32) * att_ref[:, at : at + PAIR].astype(f32)).T
        delta = [
            jnp.sum(both[h * HEAD_DIM : (h + 1) * HEAD_DIM], 0, keepdims=True) for h in range(2)
        ]
        lse = [lse_ref[2 * pair + h : 2 * pair + h + 1, :] for h in range(2)]

        def step(j, sums):
            rows = pl.ds(pl.multiple_of(j * BLOCK, BLOCK), BLOCK)
            keys = kv_ref[rows, at : at + PAIR]
            values = kv_ref[rows, columns + at : columns + at + PAIR]
            seg_k = seg_k_ref[rows, :]
            new = []
            dkey = jnp.zeros((BLOCK, PAIR), f32)
            dvalue = jnp.zeros((BLOCK, PAIR), f32)
            for h in range(2):
                raw = dot(keys, queries[h], ROWS) * 0.125
                raw = masked(raw, seg_k, seg_q, (blocks_before + i - j) * BLOCK)
                probs = jnp.exp(raw - lse[h])
                dprobs = dot(values, upstream[h], ROWS)
                dscores = (probs * (dprobs - delta[h])).astype(bf16)
                dvalue += dot(probs.astype(bf16), upstream[h])
                dkey += dot(dscores, queries[h])
                turned = k_turned[at + h * HEAD_DIM : at + (h + 1) * HEAD_DIM, rows]
                new.append(sums[h] + dot(turned, dscores))
            dkv_ref[rows, at : at + PAIR] += 0.125 * dkey
            dkv_ref[rows, columns + at : columns + at + PAIR] += dvalue
            return tuple(new)

        start = jnp.zeros((HEAD_DIM, BLOCK), f32)
        sums = lax.fori_loop(low, high, step, (start, start))
        dquery = 0.125 * jnp.concatenate(sums, 0).T
        (turned,) = turn(dquery, cos_ref[...], -sin_ref[...])
        dq_ref[:, at : at + PAIR] = turned.astype(bf16)


def attend_back(low, query, kv_all, seg_col, seg_row, lse, attended, dattended, cosine, sine):
    rows, columns = query.shape
    keys = kv_all.shape[0]
    heads = columns // HEAD_DIM
    whole = lambda i, low: (0, 0)
    block = pl.BlockSpec((BLOCK, columns), lambda i, low: (i, 0))
    table = pl.BlockSpec((BLOCK, PAIR), lambda i, low: (i, 0))
    return pl.pallas_call(
        functools.partial(attend_back_kernel, (keys - rows) // BLOCK),
        grid_spec=pltpu.PrefetchScalarGridSpec(
            num_scalar_prefetch=1,
            grid=(rows // BLOCK,),
            in_specs=[
                block,
                pl.BlockSpec((keys, 2 * columns), whole),
                pl.BlockSpec((keys, 1), whole),
                pl.BlockSpec((1, BLOCK), lambda i, low: (0, i)),
                pl.BlockSpec((heads, BLOCK), lambda i, low: (0, i)),
                block,
                block,
                table,
                table,
            ],
            out_specs=[block, pl.BlockSpec((keys, 2 * columns), whole)],
            scratch_shapes=[pltpu.VMEM((columns, keys), bf16)],
        ),
        out_shape=[
            jax.ShapeDtypeStruct((rows, columns), bf16),
            jax.ShapeDtypeStruct((keys, 2 * columns), f32),
        ],
        compiler_params=pltpu.CompilerParams(vmem_limit_bytes=VMEM),
        cost_estimate=pl.CostEstimate(
            flops=5 * rows * keys * columns,
            bytes_accessed=2 * (4 * rows * columns + 2 * keys * columns) + 8 * keys * columns,
            transcendentals=rows * keys * heads // 4,
        ),
        name="attend_back",
    )(low, query, kv_all, seg_col, seg_row, lse, attended, dattended, cosine, sine)


def join_kernel(dq_ref, own_ref, got_ref, cos_ref, sin_ref, out_ref):
    columns = dq_ref.shape[1]
    out_ref[:, :columns] = dq_ref[...]
    total = own_ref[...] + got_ref[...]
    for at, part in enumerate(turn(total[:, :columns], cos_ref[...], -sin_ref[...])):
        start = columns + at * PAIR
        out_ref[:, start : start + PAIR] = part.astype(bf16)
    out_ref[:, 2 * columns :] = total[:, columns:].astype(bf16)


def join(dquery, dkv_all, got, cosine, sine):
    rows, columns = dquery.shape
    before = (dkv_all.shape[0] - rows) // BLOCK
    return pl.pallas_call(
        join_kernel,
        grid=(rows // BLOCK,),
        in_specs=[
            pl.BlockSpec((BLOCK, columns), lambda i: (i, 0)),
            pl.BlockSpec((BLOCK, 2 * columns), lambda i: (before + i, 0)),
            pl.BlockSpec((BLOCK, 2 * columns), lambda i: (i, 0)),
            pl.BlockSpec((BLOCK, PAIR), lambda i: (i, 0)),
            pl.BlockSpec((BLOCK, PAIR), lambda i: (i, 0)),
        ],
        out_specs=pl.BlockSpec((BLOCK, 3 * columns), lambda i: (i, 0)),
        out_shape=jax.ShapeDtypeStruct((rows, 3 * columns), bf16),
        compiler_params=pltpu.CompilerParams(vmem_limit_bytes=VMEM),
        cost_estimate=pl.CostEstimate(
            flops=10 * rows * columns, bytes_accessed=24 * rows * columns, transcendentals=0
        ),
        name="join_dproj",
    )(dquery, dkv_all, got, cosine, sine)


def adamw(weight, gradient, moment, square, step_size):
    moment_new = beta_one * moment + (1.0 - beta_one) * gradient
    square_new = beta_two * square + (1.0 - beta_two) * gradient * gradient
    moment_hat = moment_new / (1.0 - beta_one**STEP)
    square_hat = square_new / (1.0 - beta_two**STEP)
    weight_new = weight - step_size * (
        moment_hat / (jnp.sqrt(square_hat) + adam_eps) + decay_rate * weight
    )
    return (weight_new, moment_new, square_new)


def adam_kernel(step_size, g_ref, w_ref, m_ref, s_ref, go_ref, wo_ref, mo_ref, so_ref):
    gradient = g_ref[...].astype(f32)
    weight, moment, square = adamw(w_ref[0], gradient, m_ref[0], s_ref[0], step_size)
    go_ref[0] = gradient
    wo_ref[0] = weight
    mo_ref[0] = moment
    so_ref[0] = square


def adam(gradient, weight, moment, square, step_size):
    flat = weight.ndim == 2
    if flat:
        weight, moment, square = weight[None], moment[None], square[None]
    count, rows, columns = weight.shape
    tall = min(rows, max(16, 131072 // columns))
    block = pl.BlockSpec((1, tall, columns), lambda j, i: (j, i, 0))
    made = pl.pallas_call(
        functools.partial(adam_kernel, step_size),
        grid=(count, rows // tall),
        in_specs=[pl.BlockSpec((tall, columns), lambda j, i: (i, j)), block, block, block],
        out_specs=[block] * 4,
        out_shape=[jax.ShapeDtypeStruct(weight.shape, f32)] * 4,
        compiler_params=pltpu.CompilerParams(vmem_limit_bytes=VMEM),
        cost_estimate=pl.CostEstimate(
            flops=15 * weight.size, bytes_accessed=30 * weight.size, transcendentals=weight.size
        ),
        name="adamw",
    )(gradient, weight, moment, square)
    return [one[0] for one in made] if flat else made


def side_by_side(weight):
    return jnp.concatenate([weight[j].astype(bf16) for j in range(weight.shape[0])], 1)


def local(
    block_input,
    segment_ids,
    positions,
    out_cotangent,
    norm_gains,
    qkv_weight,
    outproj_weight,
    gateup_weight,
    down_weight,
    moment_norm,
    moment_qkv,
    moment_outproj,
    moment_gateup,
    moment_down,
    square_norm,
    square_qkv,
    square_outproj,
    square_gateup,
    square_down,
):
    seqs_here, tok_here, width = block_input.shape
    assert seqs_here == 1 and tok_here % BLOCK == 0 and lax.axis_size("ctx") == 2
    ranks = lax.axis_size("tp")
    assert ranks & (ranks - 1) == 0
    rank = lax.axis_index("tp")
    half = lax.axis_index("ctx")
    rows_all = tok_here
    share = rows_all // ranks
    rows_axes = ("fsdp", "ctx")

    def part(values, k):
        return lax.dynamic_slice_in_dim(values, (rank ^ k) * share, share, 0)

    def swap(values, k):
        return lax.ppermute(values, "tp", [(i, i ^ k) for i in range(ranks)])

    order = sorted(range(1, ranks), key=lambda k: -bin(k).count("1"))

    def gather(own):
        got = {k: swap(own, k) for k in order}
        return [own] + [got[k] for k in range(1, ranks)]

    def natural(shares):
        whole = jnp.zeros((rows_all,) + shares[0].shape[1:], shares[0].dtype)
        for k, one in enumerate(shares):
            whole = lax.dynamic_update_slice_in_dim(whole, one, (rank ^ k) * share, 0)
        return whole

    def scatter(partials):
        got = {k: swap(partials[k], k) for k in order}
        total = partials[0].astype(f32)
        for k in order:
            total = total + got[k].astype(f32)
        return total

    qkv16 = lax.all_gather(side_by_side(qkv_weight), rows_axes, axis=0, tiled=True)
    outproj16 = lax.all_gather(outproj_weight.astype(bf16), rows_axes, axis=0, tiled=True)
    gateup16 = lax.all_gather(side_by_side(gateup_weight), rows_axes, axis=0, tiled=True)
    down16 = lax.all_gather(down_weight.astype(bf16), rows_axes, axis=0, tiled=True)
    gains16 = lax.all_gather(norm_gains.astype(bf16), rows_axes, axis=1, tiled=True)
    gain_attn = gains16[0].astype(f32)
    gain_mlp = gains16[1].astype(f32)
    columns = outproj16.shape[1]

    seg_own = segment_ids.reshape(rows_all)
    seg_prev = lax.ppermute(seg_own, "ctx", [(0, 1)])
    seg_prev = jnp.where(half == 0, -1, seg_prev)
    seg_all = jnp.concatenate([seg_prev, seg_own])
    last_of_keys = seg_all.reshape(-1, BLOCK)[:, -1]
    first_of_queries = seg_own.reshape(-1, BLOCK)[:, 0]
    low = jnp.sum(
        (last_of_keys[None, :] < first_of_queries[:, None]).astype(jnp.int32), 1, dtype=jnp.int32
    )
    seg_col = seg_all[:, None]
    seg_row = seg_own[None, :]
    cosine, sine = rope_tables(positions.reshape(rows_all))

    tokens16 = block_input.reshape(rows_all, width)
    cotan16 = out_cotangent.reshape(rows_all, width)
    normed_one, _ = normalize(tokens16.astype(f32))
    act_one = (normed_one * gain_attn).astype(bf16)
    projected = project(act_one, qkv16, cosine, sine)
    query16 = projected[:, :columns]
    kv_own = projected[:, columns:]
    kv_prev = lax.ppermute(kv_own, "ctx", [(0, 1)])
    kv_all = jnp.concatenate([kv_prev, kv_own], 0)
    attended16, lse = attend(low, query16, kv_all, seg_col, seg_row)
    attn_parts = [
        dot(part(attended16, k), outproj16, ROWS).astype(bf16) for k in range(ranks)
    ]
    own_tokens = part(tokens16, 0).astype(f32)
    resid = own_tokens + scatter(attn_parts)

    normed_two, scale_two = normalize(resid)
    act_two = jnp.concatenate(gather((normed_two * gain_mlp).astype(bf16)), 0)
    cotan_mixed = jnp.concatenate([part(cotan16, k) for k in range(ranks)], 0)
    gate_up = dot(act_two, gateup16)
    hidden = down16.shape[1]
    gate_pre = gate_up[:, :hidden]
    up_pre = gate_up[:, hidden:]
    sigma = jax.nn.sigmoid(gate_pre)
    inner16 = (gate_pre * sigma * up_pre).astype(bf16)
    down_local = dot(cotan_mixed, inner16, OVER).astype(bf16)
    down_grad = lax.psum_scatter(down_local, rows_axes, scatter_dimension=0, tiled=True)
    dinner = dot(cotan_mixed, down16)
    dgate16 = (dinner * up_pre * sigma * (1.0 + gate_pre * (1.0 - sigma))).astype(bf16)
    dup16 = (dinner * gate_pre * sigma).astype(bf16)
    dgateup16 = jnp.concatenate([dgate16, dup16], 1)
    gateup_local = dot(act_two, dgateup16, OVER).astype(bf16)
    gateup_grad = lax.psum_scatter(gateup_local, rows_axes, scatter_dimension=0, tiled=True)

    def by_share(values):
        return [values[k * share : (k + 1) * share] for k in range(ranks)]

    dact_partial = dot(dgateup16, gateup16, ROWS).astype(bf16)
    dact_two = scatter(by_share(dact_partial))
    dnorm_two, gain_two = norm_back(dact_two, normed_two, scale_two, gain_mlp)
    dresid = part(cotan16, 0).astype(f32) + dnorm_two
    dresid16 = natural(gather(dresid.astype(bf16)))

    dattended16 = dot(dresid16, outproj16).astype(bf16)
    outproj_local = dot(dresid16, attended16, OVER).astype(bf16)
    outproj_grad = lax.psum_scatter(outproj_local, rows_axes, scatter_dimension=0, tiled=True)
    dquery16, dkv_all = attend_back(
        low, query16, kv_all, seg_col, seg_row, lse, attended16, dattended16, cosine, sine
    )
    dkv_got = lax.ppermute(dkv_all[:rows_all], "ctx", [(1, 0)])
    dproj16 = join(dquery16, dkv_all, dkv_got, cosine, sine)
    qkv_local = dot(act_one, dproj16, OVER).astype(bf16)
    qkv_grad = lax.psum_scatter(qkv_local, rows_axes, scatter_dimension=0, tiled=True)
    dact_one = scatter(by_share_natural(dot(dproj16, qkv16, ROWS).astype(bf16), part, ranks))
    normed_own, scale_own = normalize(own_tokens)
    dnorm_one, gain_one = norm_back(dact_one, normed_own, scale_own, gain_attn)
    input_grad = natural(gather((dresid + dnorm_one).astype(bf16)))

    mlp_partial = dot(inner16, down16, ROWS).astype(bf16)
    out_share = resid + scatter(by_share(mlp_partial))
    block_out = natural(gather(out_share.astype(bf16)))

    gains_all = lax.psum(jnp.stack([gain_one, gain_two]), ("fsdp", "ctx", "tp"))
    wide = norm_gains.shape[1]
    place = (lax.axis_index("fsdp") * lax.axis_size("ctx") + half) * wide
    norm_grad = lax.dynamic_slice_in_dim(gains_all, place, wide, 1)

    new_norm, new_moment_norm, new_square_norm = adamw(
        norm_gains, norm_grad, moment_norm, square_norm, 0.4
    )
    down_grad, new_down, new_moment_down, new_square_down = adam(
        down_grad, down_weight, moment_down, square_down, 0.4 / math.sqrt(FF)
    )
    gateup_grad, new_gateup, new_moment_gateup, new_square_gateup = adam(
        gateup_grad, gateup_weight, moment_gateup, square_gateup, 0.4 / math.sqrt(D)
    )
    outproj_grad, new_outproj, new_moment_outproj, new_square_outproj = adam(
        outproj_grad, outproj_weight, moment_outproj, square_outproj, 0.4 / math.sqrt(D // 64)
    )
    qkv_grad, new_qkv, new_moment_qkv, new_square_qkv = adam(
        qkv_grad, qkv_weight, moment_qkv, square_qkv, 0.4 / math.sqrt(D)
    )
    return (
        block_out.reshape(block_input.shape),
        input_grad.reshape(block_input.shape),
        norm_grad,
        qkv_grad,
        outproj_grad,
        gateup_grad,
        down_grad,
        new_norm,
        new_qkv,
        new_outproj,
        new_gateup,
        new_down,
        new_moment_norm,
        new_moment_qkv,
        new_moment_outproj,
        new_moment_gateup,
        new_moment_down,
        new_square_norm,
        new_square_qkv,
        new_square_outproj,
        new_square_gateup,
        new_square_down,
    )


def by_share_natural(values, part, ranks):
    return [part(values, k) for k in range(ranks)]


def solution(mesh):
    tokens = P("fsdp", "ctx", None)
    ids = P("fsdp", "ctx")
    gains = P(None, ("fsdp", "ctx"))
    stacked = P(None, ("fsdp", "ctx"), "tp")
    single = P(("fsdp", "ctx"), "tp")
    parameters = (gains, stacked, single, stacked, single)
    return jax.shard_map(
        local,
        mesh=mesh,
        in_specs=(tokens, ids, ids, tokens) + parameters * 3,
        out_specs=(tokens, tokens) + parameters * 4,
        check_vma=False,
    )
```

```python
import functools
import math

import jax
import jax.numpy as jnp
from jax import lax
from jax.experimental import pallas as pl
from jax.experimental.pallas import tpu as pltpu
from jax.sharding import PartitionSpec as P

D = 2048
HEAD_DIM = 64
FF = 8192
STEP = 10

bf16 = jnp.bfloat16
f32 = jnp.float32

beta_one = 0.9
beta_two = 0.95
adam_eps = 1e-08
decay_rate = 0.1

BLOCK = 256
PAIR = 2 * HEAD_DIM
TILE = 256
HIDDEN = -1e30
VMEM = 56 * 1024 * 1024


def rope_tables(where_at):
    half = HEAD_DIM // 2
    freqs = jnp.exp(jnp.arange(half, dtype=f32) * (-2.0 * math.log(130000.0) / HEAD_DIM))
    angles = where_at.astype(f32)[..., None] * freqs
    cosine, sine = jnp.cos(angles), jnp.sin(angles)
    return (
        jnp.concatenate([cosine, cosine, cosine, cosine], -1),
        jnp.concatenate([-sine, sine, -sine, sine], -1),
    )


def turn(values, cosine, sine):
    columns = values.shape[1]
    lane = lax.broadcasted_iota(jnp.int32, (values.shape[0], PAIR), 1)
    low = (lane % HEAD_DIM) < HEAD_DIM // 2
    parts = []
    for at in range(0, columns, PAIR):
        tile = values[:, at : at + PAIR]
        other = jnp.where(
            low,
            pltpu.roll(tile, PAIR - HEAD_DIM // 2, 1),
            pltpu.roll(tile, HEAD_DIM // 2, 1),
        )
        parts.append(tile * cosine + other * sine)
    return parts


def normalize(values):
    scale = lax.rsqrt(jnp.mean(values * values, -1, keepdims=True) + 1e-05)
    return (values * scale, scale)


def norm_back(upstream, normed, scale, weights):
    scaled = upstream * weights
    return (
        scale * (scaled - normed * jnp.mean(scaled * normed, -1, keepdims=True)),
        jnp.sum(upstream * normed, 0),
    )


def dot(one, two, dims=((1,), (0,))):
    return lax.dot_general(one, two, (dims, ((), ())), preferred_element_type=f32)


ROWS = ((1,), (1,))
OVER = ((0,), (0,))


ANYWHERE = pl.BlockSpec(memory_space=pl.ANY)


def waiting(kernel, inputs, waits):
    def run(*refs):
        kernel(*refs[:inputs], *refs[inputs + len(waits) :])

    return run


def hold_kernel(values_ref, out_ref):
    out_ref[...] = values_ref[...]


def hold(values, *waits):
    rows, columns = values.shape
    tall = min(rows, BLOCK)
    block = pl.BlockSpec((tall, columns), lambda i: (i, 0))
    return pl.pallas_call(
        waiting(hold_kernel, 1, waits),
        grid=(rows // tall,),
        in_specs=[block] + [ANYWHERE] * len(waits),
        out_specs=block,
        out_shape=jax.ShapeDtypeStruct(values.shape, values.dtype),
        compiler_params=pltpu.CompilerParams(vmem_limit_bytes=VMEM),
        cost_estimate=pl.CostEstimate(flops=0, bytes_accessed=4 * values.size, transcendentals=0),
        name="hold",
    )(values, *waits)


def project_kernel(x_ref, w_ref, cos_ref, sin_ref, q_ref, kv_ref):
    columns = q_ref.shape[1]
    x = x_ref[...]
    for j in range(3):
        made = dot(x, w_ref[:, j * columns : (j + 1) * columns])
        if j < 2:
            for at, part in enumerate(turn(made, cos_ref[...], sin_ref[...])):
                out = q_ref if j == 0 else kv_ref
                out[:, at * PAIR : (at + 1) * PAIR] = part.astype(bf16)
        else:
            kv_ref[:, columns:] = made.astype(bf16)


def project(act, weight, wide, cosine, sine, *waits):
    rows, width = act.shape
    columns = wide // 3
    return pl.pallas_call(
        waiting(project_kernel, 4, waits),
        grid=(rows // BLOCK,),
        in_specs=[
            pl.BlockSpec((BLOCK, width), lambda i: (i, 0)),
            pl.BlockSpec((width, 3 * columns), lambda i: (0, 0)),
            pl.BlockSpec((BLOCK, PAIR), lambda i: (i, 0)),
            pl.BlockSpec((BLOCK, PAIR), lambda i: (i, 0)),
        ]
        + [ANYWHERE] * len(waits),
        out_specs=[
            pl.BlockSpec((BLOCK, columns), lambda i: (i, 0)),
            pl.BlockSpec((BLOCK, 2 * columns), lambda i: (i, 0)),
        ],
        out_shape=[
            jax.ShapeDtypeStruct((rows, columns), bf16),
            jax.ShapeDtypeStruct((rows, 2 * columns), bf16),
        ],
        compiler_params=pltpu.CompilerParams(vmem_limit_bytes=VMEM),
        cost_estimate=pl.CostEstimate(
            flops=6 * rows * width * columns,
            bytes_accessed=2 * (rows * width + 3 * width * columns + 3 * rows * columns),
            transcendentals=0,
        ),
        name="project_rope",
    )(act, weight, cosine, sine, *waits)


def head_halves(pair):
    first = lax.broadcasted_iota(jnp.int32, pair.shape, 1) < HEAD_DIM
    zero = jnp.zeros_like(pair)
    return jnp.where(first, pair, zero), jnp.where(first, zero, pair)


def block_rows(j):
    return pl.ds(pl.multiple_of(j * BLOCK, BLOCK), BLOCK)


def fetch(prev_ref, own_ref, kv, arrived):
    rows = own_ref.shape[0]
    copies = [
        pltpu.make_async_copy(prev_ref, kv.at[:rows], arrived.at[0]),
        pltpu.make_async_copy(own_ref, kv.at[rows:], arrived.at[1]),
    ]
    for copy in copies:
        copy.start()
    for copy in copies:
        copy.wait()


def attend_kernel(
    low_ref,
    q_ref,
    prev_ref,
    own_ref,
    seg_k_ref,
    seg_q_ref,
    out_ref,
    lse_ref,
    scores,
    sums,
    kv,
    v_turned,
    arrived,
):
    i = pl.program_id(0)
    columns = q_ref.shape[1]
    before = own_ref.shape[0] // BLOCK
    low = low_ref[i]
    high = before + i + 1

    @pl.when(i == 0)
    def _():
        fetch(prev_ref, own_ref, kv, arrived)

        def step(j, carry):
            rows = block_rows(j)
            v_turned[:, rows] = kv[rows, columns:].T
            return carry

        lax.fori_loop(low, 2 * before, step, 0)

    key = lax.broadcasted_iota(jnp.int32, (BLOCK, BLOCK), 0)
    query = lax.broadcasted_iota(jnp.int32, (BLOCK, BLOCK), 1)
    heads = columns // HEAD_DIM

    def score(j, tops):
        rows = block_rows(j)
        seen = (key - query <= (before + i - j) * BLOCK) & (seg_k_ref[rows, :] == seg_q_ref[...])
        bias = jnp.where(seen, 0.0, HIDDEN)
        new = []
        for at in range(0, columns, PAIR):
            keys = kv[rows, at : at + PAIR]
            for one in head_halves(q_ref[:, at : at + PAIR] * 0.125):
                h = len(new)
                raw = dot(keys, one, ROWS) + bias
                scores[h, rows, :] = raw
                new.append(jnp.maximum(tops[h], jnp.max(raw, 0, keepdims=True)))
        return tuple(new)

    tops = lax.fori_loop(low, high, score, (jnp.full((1, BLOCK), HIDDEN, f32),) * heads)

    def weigh(j, totals):
        rows = block_rows(j)
        new = []
        for h in range(heads):
            power = jnp.exp(scores[h, rows, :] - tops[h])
            scores[h, rows, :] = power
            new.append(totals[h] + jnp.sum(power, 0, keepdims=True))
        return tuple(new)

    totals = lax.fori_loop(low, high, weigh, (jnp.zeros((1, BLOCK), f32),) * heads)
    shares = tuple(1.0 / total for total in totals)
    sums[...] = jnp.zeros_like(sums)

    def mix(j, carry):
        rows = block_rows(j)
        for h in range(heads):
            probs = (scores[h, rows, :] * shares[h]).astype(bf16)
            lanes = slice(h * HEAD_DIM, (h + 1) * HEAD_DIM)
            sums[lanes, :] += dot(v_turned[lanes, rows], probs)
        return carry

    lax.fori_loop(low, high, mix, 0)
    for at in range(0, columns, PAIR):
        out_ref[:, at : at + PAIR] = sums[at : at + PAIR, :].T.astype(bf16)
    for h in range(heads):
        lse_ref[h : h + 1, :] = tops[h] + jnp.log(totals[h])


def attend(low, query, kv_prev, kv_own, seg_col, seg_row):
    rows, columns = query.shape
    keys = 2 * rows
    heads = columns // HEAD_DIM
    return pl.pallas_call(
        attend_kernel,
        grid_spec=pltpu.PrefetchScalarGridSpec(
            num_scalar_prefetch=1,
            grid=(rows // BLOCK,),
            in_specs=[
                pl.BlockSpec((BLOCK, columns), lambda i, low: (i, 0)),
                pl.BlockSpec(memory_space=pl.ANY),
                pl.BlockSpec(memory_space=pl.ANY),
                pl.BlockSpec((keys, 1), lambda i, low: (0, 0)),
                pl.BlockSpec((1, BLOCK), lambda i, low: (0, i)),
            ],
            out_specs=[
                pl.BlockSpec((BLOCK, columns), lambda i, low: (i, 0)),
                pl.BlockSpec((heads, BLOCK), lambda i, low: (0, i)),
            ],
            scratch_shapes=[
                pltpu.VMEM((heads, keys, BLOCK), f32),
                pltpu.VMEM((columns, BLOCK), f32),
                pltpu.VMEM((keys, 2 * columns), bf16),
                pltpu.VMEM((columns, keys), bf16),
                pltpu.SemaphoreType.DMA((2,)),
            ],
        ),
        out_shape=[
            jax.ShapeDtypeStruct((rows, columns), bf16),
            jax.ShapeDtypeStruct((heads, rows), f32),
        ],
        compiler_params=pltpu.CompilerParams(vmem_limit_bytes=VMEM),
        cost_estimate=pl.CostEstimate(
            flops=8 * rows * keys * columns,
            bytes_accessed=2 * (2 * rows * columns + 2 * keys * columns),
            transcendentals=rows * keys * heads // 4,
        ),
        name="attend",
    )(low, query, kv_prev, kv_own, seg_col, seg_row)


def attend_back_kernel(
    low_ref,
    q_ref,
    prev_ref,
    own_ref,
    seg_k_ref,
    seg_q_ref,
    lse_ref,
    att_ref,
    datt_ref,
    cos_ref,
    sin_ref,
    dq_ref,
    dprev_ref,
    down_ref,
    sums,
    delta,
    kv,
    k_turned,
    dkv,
    arrived,
):
    i = pl.program_id(0)
    columns = q_ref.shape[1]
    before = own_ref.shape[0] // BLOCK
    low = low_ref[i]
    high = before + i + 1

    @pl.when(i == 0)
    def _():
        fetch(prev_ref, own_ref, kv, arrived)
        dkv[...] = jnp.zeros_like(dkv)

        def step(j, carry):
            rows = block_rows(j)
            k_turned[:, rows] = kv[rows, :columns].T
            return carry

        lax.fori_loop(low, 2 * before, step, 0)

    key = lax.broadcasted_iota(jnp.int32, (BLOCK, BLOCK), 0)
    query = lax.broadcasted_iota(jnp.int32, (BLOCK, BLOCK), 1)
    for at in range(0, columns, PAIR):
        both = (datt_ref[:, at : at + PAIR].astype(f32) * att_ref[:, at : at + PAIR].astype(f32)).T
        for h in range(2):
            own = both[h * HEAD_DIM : (h + 1) * HEAD_DIM]
            at_h = at // HEAD_DIM + h
            delta[at_h : at_h + 1, :] = jnp.sum(own, 0, keepdims=True)
    sums[...] = jnp.zeros_like(sums)

    def step(j, carry):
        rows = block_rows(j)
        seen = (key - query <= (before + i - j) * BLOCK) & (seg_k_ref[rows, :] == seg_q_ref[...])
        bias = jnp.where(seen, 0.0, HIDDEN)
        for at in range(0, columns, PAIR):
            keys = kv[rows, at : at + PAIR]
            values = kv[rows, columns + at : columns + at + PAIR]
            queries = head_halves(q_ref[:, at : at + PAIR] * 0.125)
            upstream = head_halves(datt_ref[:, at : at + PAIR])
            dkey = dkv[rows, at : at + PAIR]
            dvalue = dkv[rows, columns + at : columns + at + PAIR]
            for h in range(2):
                at_h = at // HEAD_DIM + h
                lanes = slice(at_h * HEAD_DIM, (at_h + 1) * HEAD_DIM)
                raw = dot(keys, queries[h], ROWS) + bias
                probs = jnp.exp(raw - lse_ref[at_h : at_h + 1, :])
                dprobs = dot(values, upstream[h], ROWS)
                dscores = (probs * (dprobs - delta[at_h : at_h + 1, :])).astype(bf16)
                dvalue += dot(probs.astype(bf16), upstream[h])
                dkey += dot(dscores, queries[h])
                sums[lanes, :] += dot(k_turned[lanes, rows], dscores)
            dkv[rows, at : at + PAIR] = dkey
            dkv[rows, columns + at : columns + at + PAIR] = dvalue
        return carry

    lax.fori_loop(low, high, step, 0)
    for at in range(0, columns, PAIR):
        dquery = 0.125 * sums[at : at + PAIR, :].T
        (turned,) = turn(dquery, cos_ref[...], -sin_ref[...])
        dq_ref[:, at : at + PAIR] = turned.astype(bf16)

    @pl.when(i == pl.num_programs(0) - 1)
    def _():
        rows = own_ref.shape[0]
        copies = [
            pltpu.make_async_copy(dkv.at[:rows], dprev_ref, arrived.at[0]),
            pltpu.make_async_copy(dkv.at[rows:], down_ref, arrived.at[1]),
        ]
        for copy in copies:
            copy.start()
        for copy in copies:
            copy.wait()


def attend_back(
    low, query, kv_prev, kv_own, seg_col, seg_row, lse, attended, dattended, cosine, sine, *waits
):
    rows, columns = query.shape
    keys = 2 * rows
    heads = columns // HEAD_DIM
    block = pl.BlockSpec((BLOCK, columns), lambda i, low: (i, 0))
    table = pl.BlockSpec((BLOCK, PAIR), lambda i, low: (i, 0))
    anywhere = pl.BlockSpec(memory_space=pl.ANY)
    return pl.pallas_call(
        waiting(attend_back_kernel, 11, waits),
        grid_spec=pltpu.PrefetchScalarGridSpec(
            num_scalar_prefetch=1,
            grid=(rows // BLOCK,),
            in_specs=[
                block,
                anywhere,
                anywhere,
                pl.BlockSpec((keys, 1), lambda i, low: (0, 0)),
                pl.BlockSpec((1, BLOCK), lambda i, low: (0, i)),
                pl.BlockSpec((heads, BLOCK), lambda i, low: (0, i)),
                block,
                block,
                table,
                table,
            ]
            + [anywhere] * len(waits),
            out_specs=[block, anywhere, anywhere],
            scratch_shapes=[
                pltpu.VMEM((columns, BLOCK), f32),
                pltpu.VMEM((heads, BLOCK), f32),
                pltpu.VMEM((keys, 2 * columns), bf16),
                pltpu.VMEM((columns, keys), bf16),
                pltpu.VMEM((keys, 2 * columns), f32),
                pltpu.SemaphoreType.DMA((2,)),
            ],
        ),
        out_shape=[
            jax.ShapeDtypeStruct((rows, columns), bf16),
            jax.ShapeDtypeStruct((rows, 2 * columns), f32),
            jax.ShapeDtypeStruct((rows, 2 * columns), f32),
        ],
        compiler_params=pltpu.CompilerParams(vmem_limit_bytes=VMEM),
        cost_estimate=pl.CostEstimate(
            flops=12 * rows * keys * columns,
            bytes_accessed=2 * (4 * rows * columns + 2 * keys * columns) + 8 * keys * columns,
            transcendentals=rows * keys * heads // 4,
        ),
        name="attend_back",
    )(low, query, kv_prev, kv_own, seg_col, seg_row, lse, attended, dattended, cosine, sine, *waits)


def join_kernel(dq_ref, own_ref, got_ref, cos_ref, sin_ref, out_ref):
    columns = dq_ref.shape[1]
    out_ref[:, :columns] = dq_ref[...]
    total = own_ref[...] + got_ref[...]
    for at, part in enumerate(turn(total[:, :columns], cos_ref[...], -sin_ref[...])):
        start = columns + at * PAIR
        out_ref[:, start : start + PAIR] = part.astype(bf16)
    out_ref[:, 2 * columns :] = total[:, columns:].astype(bf16)


def join(dquery, dkv, got, cosine, sine, *waits):
    rows, columns = dquery.shape
    return pl.pallas_call(
        waiting(join_kernel, 5, waits),
        grid=(rows // BLOCK,),
        in_specs=[
            pl.BlockSpec((BLOCK, columns), lambda i: (i, 0)),
            pl.BlockSpec((BLOCK, 2 * columns), lambda i: (i, 0)),
            pl.BlockSpec((BLOCK, 2 * columns), lambda i: (i, 0)),
            pl.BlockSpec((BLOCK, PAIR), lambda i: (i, 0)),
            pl.BlockSpec((BLOCK, PAIR), lambda i: (i, 0)),
        ]
        + [ANYWHERE] * len(waits),
        out_specs=pl.BlockSpec((BLOCK, 3 * columns), lambda i: (i, 0)),
        out_shape=jax.ShapeDtypeStruct((rows, 3 * columns), bf16),
        compiler_params=pltpu.CompilerParams(vmem_limit_bytes=VMEM),
        cost_estimate=pl.CostEstimate(
            flops=10 * rows * columns, bytes_accessed=24 * rows * columns, transcendentals=0
        ),
        name="join_dproj",
    )(dquery, dkv, got, cosine, sine, *waits)


def pack_kernel(gateup_ref, down_ref, out_ref):
    out_ref[:, :TILE] = gateup_ref[0].astype(bf16)
    out_ref[:, TILE : 2 * TILE] = gateup_ref[1].astype(bf16)
    out_ref[:, 2 * TILE :] = down_ref[...].astype(bf16)


def pack(gateup, down, first, count):
    rows = down.shape[0]
    return pl.pallas_call(
        pack_kernel,
        grid=(count,),
        in_specs=[
            pl.BlockSpec((2, rows, TILE), lambda j: (0, 0, first + j)),
            pl.BlockSpec((rows, TILE), lambda j: (0, first + j)),
        ],
        out_specs=pl.BlockSpec((rows, 3 * TILE), lambda j: (0, j)),
        out_shape=jax.ShapeDtypeStruct((rows, 3 * TILE * count), bf16),
        compiler_params=pltpu.CompilerParams(vmem_limit_bytes=VMEM // 2),
        cost_estimate=pl.CostEstimate(
            flops=0, bytes_accessed=18 * TILE * rows * count, transcendentals=0
        ),
        name="pack_weights",
    )(gateup, down)


def hidden_kernel(act_ref, cot_ref, gate_ref, up_ref, down_ref, dgu_ref, inner_ref):
    gate = dot(act_ref[...], gate_ref[...])
    up = dot(act_ref[...], up_ref[...])
    dinner = dot(cot_ref[...], down_ref[...])
    sigma = jax.nn.sigmoid(gate)
    swish = gate * sigma
    inner_ref[...] = (swish * up).astype(bf16)
    dgu_ref[:, :TILE] = (dinner * up * sigma * (1.0 + gate * (1.0 - sigma))).astype(bf16)
    dgu_ref[:, TILE:] = (dinner * swish).astype(bf16)


def packed(width, which):
    return pl.BlockSpec((width, TILE), lambda j: (0, 3 * j + which))


def hidden(act, cotan, weights, *waits):
    rows, width = act.shape
    tiles = weights.shape[1] // (3 * TILE)
    whole = pl.BlockSpec((rows, width), lambda j: (0, 0))
    return pl.pallas_call(
        waiting(hidden_kernel, 5, waits),
        grid=(tiles,),
        in_specs=[whole, whole, packed(width, 0), packed(width, 1), packed(width, 2)]
        + [ANYWHERE] * len(waits),
        out_specs=[
            pl.BlockSpec((rows, 2 * TILE), lambda j: (0, j)),
            pl.BlockSpec((rows, TILE), lambda j: (0, j)),
        ],
        out_shape=[
            jax.ShapeDtypeStruct((rows, 2 * TILE * tiles), bf16),
            jax.ShapeDtypeStruct((rows, TILE * tiles), bf16),
        ],
        compiler_params=pltpu.CompilerParams(vmem_limit_bytes=VMEM),
        cost_estimate=pl.CostEstimate(
            flops=6 * rows * width * TILE * tiles,
            bytes_accessed=4 * rows * width + 6 * (rows + width) * TILE * tiles,
            transcendentals=rows * TILE * tiles,
        ),
        name="hidden_units",
    )(act, cotan, weights, weights, weights, *waits)


def hidden_grad_kernel(act_ref, cot_ref, dgu_ref, inner_ref, out_ref):
    out_ref[:, : 2 * TILE] = dot(act_ref[...], dgu_ref[...]).astype(bf16)
    out_ref[:, 2 * TILE :] = dot(cot_ref[...], inner_ref[...]).astype(bf16)


def hidden_grad(act_turned, cot_turned, dgu, inner, *waits):
    width, rows = act_turned.shape
    tiles = inner.shape[1] // TILE
    whole = pl.BlockSpec((width, rows), lambda j: (0, 0))
    return pl.pallas_call(
        waiting(hidden_grad_kernel, 4, waits),
        grid=(tiles,),
        in_specs=[
            whole,
            whole,
            pl.BlockSpec((rows, 2 * TILE), lambda j: (0, j)),
            pl.BlockSpec((rows, TILE), lambda j: (0, j)),
        ]
        + [ANYWHERE] * len(waits),
        out_specs=pl.BlockSpec((width, 3 * TILE), lambda j: (0, j)),
        out_shape=jax.ShapeDtypeStruct((width, 3 * TILE * tiles), bf16),
        compiler_params=pltpu.CompilerParams(vmem_limit_bytes=VMEM),
        cost_estimate=pl.CostEstimate(
            flops=6 * rows * width * TILE * tiles,
            bytes_accessed=4 * rows * width + 6 * (rows + width) * TILE * tiles,
            transcendentals=0,
        ),
        name="hidden_grad",
    )(act_turned, cot_turned, dgu, inner, *waits)


def back_kernel(at, tall, values_ref, w_ref, *refs):
    made = None
    for t in range(values_ref.shape[1] // tall):
        start = 3 * TILE * t + at
        one = dot(values_ref[:, t * tall : (t + 1) * tall], w_ref[:, start : start + tall], ROWS)
        made = one if made is None else made + one
    for ref in refs[:-1]:
        made += ref[...]
    refs[-1][...] = made.astype(refs[-1].dtype)


def back(values, weights, at, tall, start, dtype, *waits):
    rows, columns = values.shape
    width = weights.shape[0]
    wide = 2 * TILE
    block = pl.BlockSpec((rows, wide), lambda j: (0, j))
    extra = [] if start is None else [start]
    return pl.pallas_call(
        waiting(functools.partial(back_kernel, at, tall), 2 + len(extra), waits),
        grid=(width // wide,),
        in_specs=[
            pl.BlockSpec((rows, columns), lambda j: (0, 0)),
            pl.BlockSpec((wide, weights.shape[1]), lambda j: (j, 0)),
        ]
        + [block] * len(extra)
        + [ANYWHERE] * len(waits),
        out_specs=block,
        out_shape=jax.ShapeDtypeStruct((rows, width), dtype),
        compiler_params=pltpu.CompilerParams(vmem_limit_bytes=VMEM),
        cost_estimate=pl.CostEstimate(
            flops=2 * rows * width * columns,
            bytes_accessed=2 * rows * (columns + 2 * width) + 2 * width * weights.shape[1],
            transcendentals=0,
        ),
        name="from_hidden",
    )(values, weights, *extra, *waits)


def adamw(weight, gradient, moment, square, step_size):
    moment_new = beta_one * moment + (1.0 - beta_one) * gradient
    square_new = beta_two * square + (1.0 - beta_two) * gradient * gradient
    moment_hat = moment_new / (1.0 - beta_one**STEP)
    square_hat = square_new / (1.0 - beta_two**STEP)
    weight_new = weight - step_size * (
        moment_hat / (jnp.sqrt(square_hat) + adam_eps) + decay_rate * weight
    )
    return (weight_new, moment_new, square_new)


def adam_kernel(step_size, g_ref, w_ref, m_ref, s_ref, go_ref, wo_ref, mo_ref, so_ref):
    gradient = g_ref[...].astype(f32)
    weight, moment, square = adamw(w_ref[0], gradient, m_ref[0], s_ref[0], step_size)
    go_ref[0] = gradient
    wo_ref[0] = weight
    mo_ref[0] = moment
    so_ref[0] = square


def adam(gradient, first, weight, moment, square, step_size, *waits):
    flat = weight.ndim == 2
    if flat:
        weight, moment, square = weight[None], moment[None], square[None]
    count, rows, columns = weight.shape
    tall = min(rows, max(16, 131072 // columns))
    block = pl.BlockSpec((1, tall, columns), lambda j, i: (j, i, 0))
    made = pl.pallas_call(
        waiting(functools.partial(adam_kernel, step_size), 4, waits),
        grid=(count, rows // tall),
        in_specs=[pl.BlockSpec((tall, columns), lambda j, i: (i, first + j)), block, block, block]
        + [ANYWHERE] * len(waits),
        out_specs=[block] * 4,
        out_shape=[jax.ShapeDtypeStruct(weight.shape, f32)] * 4,
        compiler_params=pltpu.CompilerParams(vmem_limit_bytes=VMEM),
        cost_estimate=pl.CostEstimate(
            flops=15 * weight.size, bytes_accessed=30 * weight.size, transcendentals=weight.size
        ),
        name="adamw",
    )(gradient, weight, moment, square, *waits)
    return [one[0] for one in made] if flat else made


def adam_hidden_kernel(steps, g_ref, *refs):
    gu, down, refs = refs[:3], refs[3:6], refs[6:]
    gu_out, down_out = refs[-8:-4], refs[-4:]
    gradient = g_ref[...].astype(f32)
    for n in range(2):
        own = gradient[:, n * TILE : (n + 1) * TILE]
        weight, moment, square = adamw(gu[0][n], own, gu[1][n], gu[2][n], steps[0])
        for ref, value in zip(gu_out, (own, weight, moment, square)):
            ref[n] = value
    own = gradient[:, 2 * TILE :]
    weight, moment, square = adamw(down[0][...], own, down[1][...], down[2][...], steps[1])
    for ref, value in zip(down_out, (own, weight, moment, square)):
        ref[...] = value


def adam_hidden(gradient, gateup, down, first, filled):
    rows = gradient.shape[0]
    tiles = gradient.shape[1] // (3 * TILE)
    two = pl.BlockSpec((2, rows, TILE), lambda j: (0, 0, first + j))
    one = pl.BlockSpec((rows, TILE), lambda j: (0, first + j))
    anywhere = pl.BlockSpec(memory_space=pl.ANY)
    filled = list(filled or [])
    return pl.pallas_call(
        functools.partial(adam_hidden_kernel, (0.4 / math.sqrt(D), 0.4 / math.sqrt(FF))),
        grid=(tiles,),
        in_specs=[pl.BlockSpec((rows, 3 * TILE), lambda j: (0, j))]
        + [two] * 3
        + [one] * 3
        + [anywhere] * len(filled),
        out_specs=[two] * 4 + [one] * 4,
        out_shape=[jax.ShapeDtypeStruct(gateup[0].shape, f32)] * 4
        + [jax.ShapeDtypeStruct(down[0].shape, f32)] * 4,
        input_output_aliases={7 + n: n for n in range(len(filled))},
        compiler_params=pltpu.CompilerParams(vmem_limit_bytes=VMEM),
        cost_estimate=pl.CostEstimate(
            flops=45 * rows * TILE * tiles,
            bytes_accessed=90 * rows * TILE * tiles,
            transcendentals=3 * rows * TILE * tiles,
        ),
        name="adamw_hidden",
    )(gradient, *gateup, *down, *filled)


def side_by_side(weight):
    return jnp.concatenate([weight[j].astype(bf16) for j in range(weight.shape[0])], 1)


def edges(rows, parts):
    return [rows * n // parts // 16 * 16 for n in range(parts)] + [rows]


def exchange(values, axis, bit):
    size = lax.axis_size(axis)
    return lax.ppermute(values, axis, [(i, i ^ bit) for i in range(size)])


def bits_of(axis):
    return [1 << n for n in range(lax.axis_size(axis).bit_length() - 1)]


def turns(bits):
    return [bits[n:] + bits[:n] for n in range(len(bits))]


def gather(own, arrived=None):
    bits = bits_of("tp")
    cut = edges(own.shape[0], len(bits))
    held = []
    for n, order in enumerate(turns(bits)):
        held.append(({0: own[cut[n] : cut[n + 1]]}, order))
    for step in range(len(bits)):
        for have, order in held:
            bit = order[step]
            got = {k ^ bit: exchange(v, "tp", bit) for k, v in list(have.items())}
            have.update(got)
            if arrived is not None:
                arrived.setdefault(step, []).extend(got.values())
    return [[have[k] for have, _ in held] for k in range(lax.axis_size("tp"))]


def scatter(partials, arrived=None):
    bits = bits_of("tp")
    cut = edges(partials[0].shape[0], len(bits))
    held = []
    for n, order in enumerate(turns(bits)):
        held.append((dict(enumerate(p[cut[n] : cut[n + 1]] for p in partials)), order))
    for step in range(len(bits)):
        for have, order in held:
            bit = order[step]
            for k in [k for k in have if k & bit]:
                got = exchange(have.pop(k).astype(bf16), "tp", bit)
                if arrived is not None:
                    arrived.setdefault(step, []).append(got)
                have[k ^ bit] = have[k ^ bit].astype(f32) + got.astype(f32)
    return jnp.concatenate([have[0] for have, _ in held], 0)


def to_partners(pieces):
    order = sorted(range(1, len(pieces)), key=lambda k: -bin(k).count("1"))
    got = {k: exchange(pieces[k], "tp", k) for k in order}
    return [pieces[0]] + [got[k] for k in range(1, len(pieces))]


def sum_everywhere(values):
    for axis in ("tp", "ctx", "fsdp"):
        for bit in bits_of(axis):
            values = values + exchange(values, axis, bit)
    return values


def residual_kernel(ranks, att_ref, x_ref, gain_ref, *refs):
    weights, (resid_ref, act_ref, scale_ref) = refs[:-3], refs[-3:]
    columns = att_ref.shape[1] // ranks
    parts = len(weights) // ranks
    made = []
    for n in range(parts):
        one = None
        for k in range(ranks):
            att = att_ref[:, k * columns : (k + 1) * columns]
            more = dot(att, weights[k * parts + n][...], ROWS)
            one = more if one is None else one + more
        made.append(one)
    resid = jnp.concatenate(made, 1) + x_ref[...].astype(f32)
    normed, scale = normalize(resid)
    resid_ref[...] = resid
    act_ref[...] = (normed * gain_ref[...]).astype(bf16)
    scale_ref[...] = scale


def residual(attended, tokens, gain, weights):
    rows, width = tokens.shape
    flat = [piece for pieces in weights for piece in pieces]
    return pl.pallas_call(
        functools.partial(residual_kernel, len(weights)),
        out_shape=[
            jax.ShapeDtypeStruct((rows, width), f32),
            jax.ShapeDtypeStruct((rows, width), bf16),
            jax.ShapeDtypeStruct((rows, 1), f32),
        ],
        compiler_params=pltpu.CompilerParams(vmem_limit_bytes=VMEM),
        cost_estimate=pl.CostEstimate(
            flops=2 * rows * width * width,
            bytes_accessed=2 * width * width + 12 * rows * width,
            transcendentals=0,
        ),
        name="residual",
    )(attended, tokens, gain, *flat)


def attended_back_kernel(ranks, d_ref, *refs):
    weights, outs = refs[:-ranks], refs[-ranks:]
    parts = len(weights) // ranks
    for k in range(ranks):
        one = None
        at = 0
        for n in range(parts):
            weight = weights[k * parts + n][...]
            more = dot(d_ref[:, at : at + weight.shape[0]], weight)
            at += weight.shape[0]
            one = more if one is None else one + more
        outs[k][...] = one.astype(bf16)


def attended_back(dresid, weights, *waits):
    rows, width = dresid.shape
    flat = [piece for pieces in weights for piece in pieces]
    return pl.pallas_call(
        waiting(functools.partial(attended_back_kernel, len(weights)), 1 + len(flat), waits),
        in_specs=[pl.BlockSpec(memory_space=pltpu.VMEM)] * (1 + len(flat)) + [ANYWHERE] * len(waits),
        out_shape=[jax.ShapeDtypeStruct((rows, one[0].shape[1]), bf16) for one in weights],
        compiler_params=pltpu.CompilerParams(vmem_limit_bytes=VMEM),
        cost_estimate=pl.CostEstimate(
            flops=2 * rows * width * width,
            bytes_accessed=2 * width * width + 4 * rows * width,
            transcendentals=0,
        ),
        name="attended_back",
    )(dresid, *flat, *waits)


def local(
    block_input,
    segment_ids,
    positions,
    out_cotangent,
    norm_gains,
    qkv_weight,
    outproj_weight,
    gateup_weight,
    down_weight,
    moment_norm,
    moment_qkv,
    moment_outproj,
    moment_gateup,
    moment_down,
    square_norm,
    square_qkv,
    square_outproj,
    square_gateup,
    square_down,
):
    seqs_here, tok_here, width = block_input.shape
    ranks = lax.axis_size("tp")
    assert seqs_here == 1 and tok_here % BLOCK == 0 and lax.axis_size("ctx") == 2
    assert all(lax.axis_size(axis) & (lax.axis_size(axis) - 1) == 0 for axis in ("tp", "fsdp"))
    rank = lax.axis_index("tp")
    half = lax.axis_index("ctx")
    rows_all = tok_here
    share = rows_all // ranks
    rows_axes = ("fsdp", "ctx")
    tiles = down_weight.shape[1] // TILE
    early = 5 * tiles // 8
    cuts = [(0, early), (early, tiles - early)]

    def part(values, k):
        return lax.dynamic_slice_in_dim(values, (rank ^ k) * share, share, 0)

    def mixed(values):
        return jnp.concatenate([part(values, k) for k in range(ranks)], 0)

    def natural(shares):
        first = shares[0][0]
        whole = jnp.zeros((rows_all,) + first.shape[1:], first.dtype)
        for k, pieces in enumerate(shares):
            at = (rank ^ k) * share
            for piece in pieces:
                whole = lax.dynamic_update_slice_in_dim(whole, piece, at, 0)
                at = at + piece.shape[0]
        return whole

    def flat(shares):
        return jnp.concatenate([piece for pieces in shares for piece in pieces], 0)

    def by_share(values):
        return [values[k * share : (k + 1) * share] for k in range(ranks)]

    attn16 = jnp.concatenate([side_by_side(qkv_weight), outproj_weight.astype(bf16)], 1)
    attn16 = lax.all_gather(attn16, rows_axes, axis=0, tiled=True)
    mlp16 = [
        lax.all_gather(
            pack(gateup_weight, down_weight, first, count), rows_axes, axis=0, tiled=True
        )
        for first, count in cuts
    ]
    gains16 = lax.all_gather(norm_gains.astype(bf16), rows_axes, axis=1, tiled=True)
    gain_attn = gains16[0].astype(f32)
    gain_mlp = gains16[1].astype(f32)
    columns = outproj_weight.shape[1]
    outproj_all = gather(attn16[:, 3 * columns :])

    seg_own = segment_ids.reshape(rows_all)
    seg_prev = lax.ppermute(seg_own, "ctx", [(0, 1)])
    seg_prev = jnp.where(half == 0, -1, seg_prev)
    seg_all = jnp.concatenate([seg_prev, seg_own])
    last_of_keys = seg_all.reshape(-1, BLOCK)[:, -1]
    first_of_queries = seg_own.reshape(-1, BLOCK)[:, 0]
    low = jnp.sum(
        (last_of_keys[None, :] < first_of_queries[:, None]).astype(jnp.int32), 1, dtype=jnp.int32
    )
    seg_col = seg_all[:, None]
    seg_row = seg_own[None, :]
    cosine, sine = rope_tables(positions.reshape(rows_all))

    tokens16 = block_input.reshape(rows_all, width)
    cotan16 = out_cotangent.reshape(rows_all, width)
    cotan_mixed = mixed(cotan16)
    cotan_turned = cotan_mixed.T
    normed_one, _ = normalize(tokens16.astype(f32))
    act_one = (normed_one * gain_attn).astype(bf16)
    query16, kv_own = project(act_one, attn16, 3 * columns, cosine, sine, cotan_turned)
    kv_prev = lax.ppermute(kv_own, "ctx", [(0, 1)])
    attended16, lse = attend(low, query16, kv_prev, kv_own, seg_col, seg_row)
    attended_own = jnp.concatenate(to_partners([part(attended16, k) for k in range(ranks)]), 1)
    own_tokens = part(tokens16, 0).astype(f32)
    resid, act_share, scale_two = residual(
        attended_own, part(tokens16, 0), gain_mlp[None], outproj_all
    )

    act_two = flat(gather(act_share))
    act_turned = act_two.T
    dact = made = None
    hidden_grads = []
    for n, weights in enumerate(mlp16):
        last = n == len(mlp16) - 1
        dtype = bf16 if last else f32
        dgu, inner = hidden(act_two, cotan_mixed, weights, *([] if dact is None else [dact]))
        if last:
            dact = back(dgu, weights, 0, 2 * TILE, dact, dtype)
            local_grad = hidden_grad(act_turned, cotan_turned, dgu, inner, dact)
        else:
            local_grad = hidden_grad(act_turned, cotan_turned, dgu, inner)
            dact = back(dgu, weights, 0, 2 * TILE, dact, dtype, local_grad)
        hidden_grads.append(
            lax.psum_scatter(local_grad, rows_axes, scatter_dimension=0, tiled=True)
        )
        made = back(inner, weights, 2 * TILE, TILE, made, dtype, local_grad)

    dact_two = scatter(by_share(dact))
    normed_two = resid * scale_two
    dnorm_two, gain_two = norm_back(dact_two, normed_two, scale_two, gain_mlp)
    dresid = part(cotan16, 0).astype(f32) + dnorm_two
    dresid16 = dresid.astype(bf16)

    pieces = to_partners(attended_back(dresid16, outproj_all))
    dattended16 = natural([[piece] for piece in pieces])
    dresid_mixed = flat(gather(dresid16))
    dquery16, dkv_prev, dkv_own = attend_back(
        low,
        query16,
        kv_prev,
        kv_own,
        seg_col,
        seg_row,
        lse,
        attended16,
        dattended16,
        cosine,
        sine,
        dresid_mixed,
        made,
    )
    gateup_state = (gateup_weight, moment_gateup, square_gateup)
    down_state = (down_weight, moment_down, square_down)
    filled = adam_hidden(hidden_grads[0], gateup_state, down_state, 0, None)
    dkv_got = lax.ppermute(dkv_prev, "ctx", [(1, 0)])
    outproj_local = dot(dresid_mixed, mixed(attended16), OVER).astype(bf16)
    dproj16 = join(dquery16, dkv_own, dkv_got, cosine, sine, outproj_local, filled[0])
    qkv_local = dot(act_one, dproj16, OVER).astype(bf16)
    attn_grad = lax.psum_scatter(
        jnp.concatenate([qkv_local, outproj_local], 1), rows_axes, scatter_dimension=0, tiled=True
    )
    out_share = resid + scatter(by_share(hold(made, dproj16)))
    dact_one = scatter(
        [dot(part(dproj16, k), attn16[:, : 3 * columns], ROWS).astype(bf16) for k in range(ranks)]
    )
    normed_own, scale_own = normalize(own_tokens)
    dnorm_one, gain_one = norm_back(dact_one, normed_own, scale_own, gain_attn)
    for (first, _), gradient in zip(cuts[1:], hidden_grads[1:]):
        filled = adam_hidden(gradient, gateup_state, down_state, first, filled)

    arrived = {}
    input_grad = natural(gather((dresid + dnorm_one).astype(bf16), arrived))
    block_out = natural(gather(hold(out_share.astype(bf16), filled[0], *arrived[0])))

    gateup_grad, new_gateup, new_moment_gateup, new_square_gateup = filled[:4]
    down_grad, new_down, new_moment_down, new_square_down = filled[4:]
    outproj_grad, new_outproj, new_moment_outproj, new_square_outproj = adam(
        attn_grad,
        3,
        outproj_weight,
        moment_outproj,
        square_outproj,
        0.4 / math.sqrt(D // 64),
        new_down,
    )
    qkv_grad, new_qkv, new_moment_qkv, new_square_qkv = adam(
        attn_grad, 0, qkv_weight, moment_qkv, square_qkv, 0.4 / math.sqrt(D), new_down
    )
    gains_all = sum_everywhere(hold(jnp.stack([gain_one, gain_two]), new_qkv, new_outproj))
    wide = norm_gains.shape[1]
    place = (lax.axis_index("fsdp") * lax.axis_size("ctx") + half) * wide
    norm_grad = lax.dynamic_slice_in_dim(gains_all, place, wide, 1)

    new_norm, new_moment_norm, new_square_norm = adamw(
        norm_gains, norm_grad, moment_norm, square_norm, 0.4
    )
    return (
        block_out.reshape(block_input.shape),
        input_grad.reshape(block_input.shape),
        norm_grad,
        qkv_grad,
        outproj_grad,
        gateup_grad,
        down_grad,
        new_norm,
        new_qkv,
        new_outproj,
        new_gateup,
        new_down,
        new_moment_norm,
        new_moment_qkv,
        new_moment_outproj,
        new_moment_gateup,
        new_moment_down,
        new_square_norm,
        new_square_qkv,
        new_square_outproj,
        new_square_gateup,
        new_square_down,
    )


def solution(mesh):
    tokens = P("fsdp", "ctx", None)
    ids = P("fsdp", "ctx")
    gains = P(None, ("fsdp", "ctx"))
    stacked = P(None, ("fsdp", "ctx"), "tp")
    single = P(("fsdp", "ctx"), "tp")
    parameters = (gains, stacked, single, stacked, single)
    return jax.shard_map(
        local,
        mesh=mesh,
        in_specs=(tokens, ids, ids, tokens) + parameters * 3,
        out_specs=(tokens, tokens) + parameters * 4,
        check_vma=False,
    )
```

```python
import functools
import math

import jax
import jax.numpy as jnp
from jax import lax
from jax.experimental import pallas as pl
from jax.experimental.pallas import tpu as pltpu
from jax.sharding import PartitionSpec as P

D = 2048
HEAD_DIM = 64
FF = 8192
STEP = 10

bf16 = jnp.bfloat16
f32 = jnp.float32

beta_one = 0.9
beta_two = 0.95
adam_eps = 1e-08
decay_rate = 0.1

BLOCK = 256
PAIR = 2 * HEAD_DIM
TILE = 256
HIDDEN = -1e30
VMEM = 56 * 1024 * 1024


def rope_tables(where_at):
    half = HEAD_DIM // 2
    freqs = jnp.exp(jnp.arange(half, dtype=f32) * (-2.0 * math.log(130000.0) / HEAD_DIM))
    angles = where_at.astype(f32)[..., None] * freqs
    cosine, sine = jnp.cos(angles), jnp.sin(angles)
    return (
        jnp.concatenate([cosine, cosine, cosine, cosine], -1),
        jnp.concatenate([-sine, sine, -sine, sine], -1),
    )


def turn(values, cosine, sine):
    columns = values.shape[1]
    lane = lax.broadcasted_iota(jnp.int32, (values.shape[0], PAIR), 1)
    low = (lane % HEAD_DIM) < HEAD_DIM // 2
    parts = []
    for at in range(0, columns, PAIR):
        tile = values[:, at : at + PAIR]
        other = jnp.where(
            low,
            pltpu.roll(tile, PAIR - HEAD_DIM // 2, 1),
            pltpu.roll(tile, HEAD_DIM // 2, 1),
        )
        parts.append(tile * cosine + other * sine)
    return parts


def normalize(values):
    scale = lax.rsqrt(jnp.mean(values * values, -1, keepdims=True) + 1e-05)
    return (values * scale, scale)


def norm_back(upstream, normed, scale, weights):
    scaled = upstream * weights
    return (
        scale * (scaled - normed * jnp.mean(scaled * normed, -1, keepdims=True)),
        jnp.sum(upstream * normed, 0),
    )


def dot(one, two, dims=((1,), (0,))):
    return lax.dot_general(one, two, (dims, ((), ())), preferred_element_type=f32)


ROWS = ((1,), (1,))
OVER = ((0,), (0,))


ANYWHERE = pl.BlockSpec(memory_space=pl.ANY)


def waiting(kernel, inputs, waits):
    def run(*refs):
        kernel(*refs[:inputs], *refs[inputs + len(waits) :])

    return run


def hold_kernel(values_ref, out_ref):
    out_ref[...] = values_ref[...]


def hold(values, *waits):
    rows, columns = values.shape
    tall = min(rows, BLOCK)
    block = pl.BlockSpec((tall, columns), lambda i: (i, 0))
    return pl.pallas_call(
        waiting(hold_kernel, 1, waits),
        grid=(rows // tall,),
        in_specs=[block] + [ANYWHERE] * len(waits),
        out_specs=block,
        out_shape=jax.ShapeDtypeStruct(values.shape, values.dtype),
        compiler_params=pltpu.CompilerParams(vmem_limit_bytes=VMEM),
        cost_estimate=pl.CostEstimate(flops=0, bytes_accessed=4 * values.size, transcendentals=0),
        name="hold",
    )(values, *waits)


def project_kernel(x_ref, w_ref, cos_ref, sin_ref, q_ref, kv_ref):
    columns = q_ref.shape[1]
    x = x_ref[...]
    for j in range(3):
        made = dot(x, w_ref[:, j * columns : (j + 1) * columns])
        if j < 2:
            for at, part in enumerate(turn(made, cos_ref[...], sin_ref[...])):
                out = q_ref if j == 0 else kv_ref
                out[:, at * PAIR : (at + 1) * PAIR] = part.astype(bf16)
        else:
            kv_ref[:, columns:] = made.astype(bf16)


def project(act, weight, wide, cosine, sine, *waits):
    rows, width = act.shape
    columns = wide // 3
    return pl.pallas_call(
        waiting(project_kernel, 4, waits),
        grid=(rows // BLOCK,),
        in_specs=[
            pl.BlockSpec((BLOCK, width), lambda i: (i, 0)),
            pl.BlockSpec((width, 3 * columns), lambda i: (0, 0)),
            pl.BlockSpec((BLOCK, PAIR), lambda i: (i, 0)),
            pl.BlockSpec((BLOCK, PAIR), lambda i: (i, 0)),
        ]
        + [ANYWHERE] * len(waits),
        out_specs=[
            pl.BlockSpec((BLOCK, columns), lambda i: (i, 0)),
            pl.BlockSpec((BLOCK, 2 * columns), lambda i: (i, 0)),
        ],
        out_shape=[
            jax.ShapeDtypeStruct((rows, columns), bf16),
            jax.ShapeDtypeStruct((rows, 2 * columns), bf16),
        ],
        compiler_params=pltpu.CompilerParams(vmem_limit_bytes=VMEM),
        cost_estimate=pl.CostEstimate(
            flops=6 * rows * width * columns,
            bytes_accessed=2 * (rows * width + 3 * width * columns + 3 * rows * columns),
            transcendentals=0,
        ),
        name="project_rope",
    )(act, weight, cosine, sine, *waits)


def head_halves(pair):
    first = lax.broadcasted_iota(jnp.int32, pair.shape, 1) < HEAD_DIM
    zero = jnp.zeros_like(pair)
    return jnp.where(first, pair, zero), jnp.where(first, zero, pair)


def block_rows(j):
    return pl.ds(pl.multiple_of(j * BLOCK, BLOCK), BLOCK)


def fetch(prev_ref, own_ref, kv, arrived):
    rows = own_ref.shape[0]
    copies = [
        pltpu.make_async_copy(prev_ref, kv.at[:rows], arrived.at[0]),
        pltpu.make_async_copy(own_ref, kv.at[rows:], arrived.at[1]),
    ]
    for copy in copies:
        copy.start()
    for copy in copies:
        copy.wait()


def attend_kernel(
    low_ref,
    q_ref,
    prev_ref,
    own_ref,
    seg_k_ref,
    seg_q_ref,
    out_ref,
    lse_ref,
    scores,
    sums,
    kv,
    v_turned,
    arrived,
):
    i = pl.program_id(0)
    columns = q_ref.shape[1]
    before = own_ref.shape[0] // BLOCK
    low = low_ref[i]
    high = before + i + 1

    @pl.when(i == 0)
    def _():
        fetch(prev_ref, own_ref, kv, arrived)

        def step(j, carry):
            rows = block_rows(j)
            v_turned[:, rows] = kv[rows, columns:].T
            return carry

        lax.fori_loop(low, 2 * before, step, 0)

    key = lax.broadcasted_iota(jnp.int32, (BLOCK, BLOCK), 0)
    query = lax.broadcasted_iota(jnp.int32, (BLOCK, BLOCK), 1)
    heads = columns // HEAD_DIM

    def score(j, tops):
        rows = block_rows(j)
        seen = (key - query <= (before + i - j) * BLOCK) & (seg_k_ref[rows, :] == seg_q_ref[...])
        bias = jnp.where(seen, 0.0, HIDDEN)
        new = []
        for at in range(0, columns, PAIR):
            keys = kv[rows, at : at + PAIR]
            for one in head_halves(q_ref[:, at : at + PAIR] * 0.125):
                h = len(new)
                raw = dot(keys, one, ROWS) + bias
                scores[h, rows, :] = raw
                new.append(jnp.maximum(tops[h], jnp.max(raw, 0, keepdims=True)))
        return tuple(new)

    tops = lax.fori_loop(low, high, score, (jnp.full((1, BLOCK), HIDDEN, f32),) * heads)

    def weigh(j, totals):
        rows = block_rows(j)
        new = []
        for h in range(heads):
            power = jnp.exp(scores[h, rows, :] - tops[h])
            scores[h, rows, :] = power
            new.append(totals[h] + jnp.sum(power, 0, keepdims=True))
        return tuple(new)

    totals = lax.fori_loop(low, high, weigh, (jnp.zeros((1, BLOCK), f32),) * heads)
    shares = tuple(1.0 / total for total in totals)
    sums[...] = jnp.zeros_like(sums)

    def mix(j, carry):
        rows = block_rows(j)
        for h in range(heads):
            probs = (scores[h, rows, :] * shares[h]).astype(bf16)
            lanes = slice(h * HEAD_DIM, (h + 1) * HEAD_DIM)
            sums[lanes, :] += dot(v_turned[lanes, rows], probs)
        return carry

    lax.fori_loop(low, high, mix, 0)
    for at in range(0, columns, PAIR):
        out_ref[:, at : at + PAIR] = sums[at : at + PAIR, :].T.astype(bf16)
    for h in range(heads):
        lse_ref[h : h + 1, :] = tops[h] + jnp.log(totals[h])


def attend(low, query, kv_prev, kv_own, seg_col, seg_row):
    rows, columns = query.shape
    keys = 2 * rows
    heads = columns // HEAD_DIM
    return pl.pallas_call(
        attend_kernel,
        grid_spec=pltpu.PrefetchScalarGridSpec(
            num_scalar_prefetch=1,
            grid=(rows // BLOCK,),
            in_specs=[
                pl.BlockSpec((BLOCK, columns), lambda i, low: (i, 0)),
                pl.BlockSpec(memory_space=pl.ANY),
                pl.BlockSpec(memory_space=pl.ANY),
                pl.BlockSpec((keys, 1), lambda i, low: (0, 0)),
                pl.BlockSpec((1, BLOCK), lambda i, low: (0, i)),
            ],
            out_specs=[
                pl.BlockSpec((BLOCK, columns), lambda i, low: (i, 0)),
                pl.BlockSpec((heads, BLOCK), lambda i, low: (0, i)),
            ],
            scratch_shapes=[
                pltpu.VMEM((heads, keys, BLOCK), f32),
                pltpu.VMEM((columns, BLOCK), f32),
                pltpu.VMEM((keys, 2 * columns), bf16),
                pltpu.VMEM((columns, keys), bf16),
                pltpu.SemaphoreType.DMA((2,)),
            ],
        ),
        out_shape=[
            jax.ShapeDtypeStruct((rows, columns), bf16),
            jax.ShapeDtypeStruct((heads, rows), f32),
        ],
        compiler_params=pltpu.CompilerParams(vmem_limit_bytes=VMEM),
        cost_estimate=pl.CostEstimate(
            flops=8 * rows * keys * columns,
            bytes_accessed=2 * (2 * rows * columns + 2 * keys * columns),
            transcendentals=rows * keys * heads // 4,
        ),
        name="attend",
    )(low, query, kv_prev, kv_own, seg_col, seg_row)


def attend_back_kernel(
    low_ref,
    q_ref,
    prev_ref,
    own_ref,
    seg_k_ref,
    seg_q_ref,
    lse_ref,
    att_ref,
    datt_ref,
    cos_ref,
    sin_ref,
    dq_ref,
    dprev_ref,
    down_ref,
    sums,
    delta,
    kv,
    k_turned,
    dkv,
    arrived,
):
    i = pl.program_id(0)
    columns = q_ref.shape[1]
    before = own_ref.shape[0] // BLOCK
    low = low_ref[i]
    high = before + i + 1

    @pl.when(i == 0)
    def _():
        fetch(prev_ref, own_ref, kv, arrived)
        dkv[...] = jnp.zeros_like(dkv)

        def step(j, carry):
            rows = block_rows(j)
            k_turned[:, rows] = kv[rows, :columns].T
            return carry

        lax.fori_loop(low, 2 * before, step, 0)

    key = lax.broadcasted_iota(jnp.int32, (BLOCK, BLOCK), 0)
    query = lax.broadcasted_iota(jnp.int32, (BLOCK, BLOCK), 1)
    for at in range(0, columns, PAIR):
        both = (datt_ref[:, at : at + PAIR].astype(f32) * att_ref[:, at : at + PAIR].astype(f32)).T
        for h in range(2):
            own = both[h * HEAD_DIM : (h + 1) * HEAD_DIM]
            at_h = at // HEAD_DIM + h
            delta[at_h : at_h + 1, :] = jnp.sum(own, 0, keepdims=True)
    sums[...] = jnp.zeros_like(sums)

    def step(j, carry):
        rows = block_rows(j)
        seen = (key - query <= (before + i - j) * BLOCK) & (seg_k_ref[rows, :] == seg_q_ref[...])
        bias = jnp.where(seen, 0.0, HIDDEN)
        for at in range(0, columns, PAIR):
            keys = kv[rows, at : at + PAIR]
            values = kv[rows, columns + at : columns + at + PAIR]
            queries = head_halves(q_ref[:, at : at + PAIR] * 0.125)
            upstream = head_halves(datt_ref[:, at : at + PAIR])
            dkey = dkv[rows, at : at + PAIR]
            dvalue = dkv[rows, columns + at : columns + at + PAIR]
            for h in range(2):
                at_h = at // HEAD_DIM + h
                lanes = slice(at_h * HEAD_DIM, (at_h + 1) * HEAD_DIM)
                raw = dot(keys, queries[h], ROWS) + bias
                probs = jnp.exp(raw - lse_ref[at_h : at_h + 1, :])
                dprobs = dot(values, upstream[h], ROWS)
                dscores = (probs * (dprobs - delta[at_h : at_h + 1, :])).astype(bf16)
                dvalue += dot(probs.astype(bf16), upstream[h])
                dkey += dot(dscores, queries[h])
                sums[lanes, :] += dot(k_turned[lanes, rows], dscores)
            dkv[rows, at : at + PAIR] = dkey
            dkv[rows, columns + at : columns + at + PAIR] = dvalue
        return carry

    lax.fori_loop(low, high, step, 0)
    for at in range(0, columns, PAIR):
        dquery = 0.125 * sums[at : at + PAIR, :].T
        (turned,) = turn(dquery, cos_ref[...], -sin_ref[...])
        dq_ref[:, at : at + PAIR] = turned.astype(bf16)

    @pl.when(i == pl.num_programs(0) - 1)
    def _():
        rows = own_ref.shape[0]
        copies = [
            pltpu.make_async_copy(dkv.at[:rows], dprev_ref, arrived.at[0]),
            pltpu.make_async_copy(dkv.at[rows:], down_ref, arrived.at[1]),
        ]
        for copy in copies:
            copy.start()
        for copy in copies:
            copy.wait()


def attend_back(
    low, query, kv_prev, kv_own, seg_col, seg_row, lse, attended, dattended, cosine, sine, *waits
):
    rows, columns = query.shape
    keys = 2 * rows
    heads = columns // HEAD_DIM
    block = pl.BlockSpec((BLOCK, columns), lambda i, low: (i, 0))
    table = pl.BlockSpec((BLOCK, PAIR), lambda i, low: (i, 0))
    anywhere = pl.BlockSpec(memory_space=pl.ANY)
    return pl.pallas_call(
        waiting(attend_back_kernel, 11, waits),
        grid_spec=pltpu.PrefetchScalarGridSpec(
            num_scalar_prefetch=1,
            grid=(rows // BLOCK,),
            in_specs=[
                block,
                anywhere,
                anywhere,
                pl.BlockSpec((keys, 1), lambda i, low: (0, 0)),
                pl.BlockSpec((1, BLOCK), lambda i, low: (0, i)),
                pl.BlockSpec((heads, BLOCK), lambda i, low: (0, i)),
                block,
                block,
                table,
                table,
            ]
            + [anywhere] * len(waits),
            out_specs=[block, anywhere, anywhere],
            scratch_shapes=[
                pltpu.VMEM((columns, BLOCK), f32),
                pltpu.VMEM((heads, BLOCK), f32),
                pltpu.VMEM((keys, 2 * columns), bf16),
                pltpu.VMEM((columns, keys), bf16),
                pltpu.VMEM((keys, 2 * columns), f32),
                pltpu.SemaphoreType.DMA((2,)),
            ],
        ),
        out_shape=[
            jax.ShapeDtypeStruct((rows, columns), bf16),
            jax.ShapeDtypeStruct((rows, 2 * columns), f32),
            jax.ShapeDtypeStruct((rows, 2 * columns), f32),
        ],
        compiler_params=pltpu.CompilerParams(vmem_limit_bytes=VMEM),
        cost_estimate=pl.CostEstimate(
            flops=12 * rows * keys * columns,
            bytes_accessed=2 * (4 * rows * columns + 2 * keys * columns) + 8 * keys * columns,
            transcendentals=rows * keys * heads // 4,
        ),
        name="attend_back",
    )(low, query, kv_prev, kv_own, seg_col, seg_row, lse, attended, dattended, cosine, sine, *waits)


def join_kernel(dq_ref, own_ref, got_ref, cos_ref, sin_ref, out_ref):
    columns = dq_ref.shape[1]
    out_ref[:, :columns] = dq_ref[...]
    total = own_ref[...] + got_ref[...]
    for at, part in enumerate(turn(total[:, :columns], cos_ref[...], -sin_ref[...])):
        start = columns + at * PAIR
        out_ref[:, start : start + PAIR] = part.astype(bf16)
    out_ref[:, 2 * columns :] = total[:, columns:].astype(bf16)


def join(dquery, dkv, got, cosine, sine, *waits):
    rows, columns = dquery.shape
    return pl.pallas_call(
        waiting(join_kernel, 5, waits),
        grid=(rows // BLOCK,),
        in_specs=[
            pl.BlockSpec((BLOCK, columns), lambda i: (i, 0)),
            pl.BlockSpec((BLOCK, 2 * columns), lambda i: (i, 0)),
            pl.BlockSpec((BLOCK, 2 * columns), lambda i: (i, 0)),
            pl.BlockSpec((BLOCK, PAIR), lambda i: (i, 0)),
            pl.BlockSpec((BLOCK, PAIR), lambda i: (i, 0)),
        ]
        + [ANYWHERE] * len(waits),
        out_specs=pl.BlockSpec((BLOCK, 3 * columns), lambda i: (i, 0)),
        out_shape=jax.ShapeDtypeStruct((rows, 3 * columns), bf16),
        compiler_params=pltpu.CompilerParams(vmem_limit_bytes=VMEM),
        cost_estimate=pl.CostEstimate(
            flops=10 * rows * columns, bytes_accessed=24 * rows * columns, transcendentals=0
        ),
        name="join_dproj",
    )(dquery, dkv, got, cosine, sine, *waits)


def pack_kernel(gateup_ref, down_ref, out_ref):
    out_ref[:, :TILE] = gateup_ref[0].astype(bf16)
    out_ref[:, TILE : 2 * TILE] = gateup_ref[1].astype(bf16)
    out_ref[:, 2 * TILE :] = down_ref[...].astype(bf16)


def pack(gateup, down, first, count):
    rows = down.shape[0]
    return pl.pallas_call(
        pack_kernel,
        grid=(count,),
        in_specs=[
            pl.BlockSpec((2, rows, TILE), lambda j: (0, 0, first + j)),
            pl.BlockSpec((rows, TILE), lambda j: (0, first + j)),
        ],
        out_specs=pl.BlockSpec((rows, 3 * TILE), lambda j: (0, j)),
        out_shape=jax.ShapeDtypeStruct((rows, 3 * TILE * count), bf16),
        compiler_params=pltpu.CompilerParams(vmem_limit_bytes=VMEM // 2),
        cost_estimate=pl.CostEstimate(
            flops=0, bytes_accessed=18 * TILE * rows * count, transcendentals=0
        ),
        name="pack_weights",
    )(gateup, down)


def hidden_kernel(act_ref, cot_ref, gate_ref, up_ref, down_ref, dgu_ref, inner_ref):
    gate = dot(act_ref[...], gate_ref[...])
    up = dot(act_ref[...], up_ref[...])
    dinner = dot(cot_ref[...], down_ref[...])
    sigma = jax.nn.sigmoid(gate)
    swish = gate * sigma
    inner_ref[...] = (swish * up).astype(bf16)
    dgu_ref[:, :TILE] = (dinner * up * sigma * (1.0 + gate * (1.0 - sigma))).astype(bf16)
    dgu_ref[:, TILE:] = (dinner * swish).astype(bf16)


def packed(width, which):
    return pl.BlockSpec((width, TILE), lambda j: (0, 3 * j + which))


def hidden(act, cotan, weights, *waits):
    rows, width = act.shape
    tiles = weights.shape[1] // (3 * TILE)
    whole = pl.BlockSpec((rows, width), lambda j: (0, 0))
    return pl.pallas_call(
        waiting(hidden_kernel, 5, waits),
        grid=(tiles,),
        in_specs=[whole, whole, packed(width, 0), packed(width, 1), packed(width, 2)]
        + [ANYWHERE] * len(waits),
        out_specs=[
            pl.BlockSpec((rows, 2 * TILE), lambda j: (0, j)),
            pl.BlockSpec((rows, TILE), lambda j: (0, j)),
        ],
        out_shape=[
            jax.ShapeDtypeStruct((rows, 2 * TILE * tiles), bf16),
            jax.ShapeDtypeStruct((rows, TILE * tiles), bf16),
        ],
        compiler_params=pltpu.CompilerParams(vmem_limit_bytes=VMEM),
        cost_estimate=pl.CostEstimate(
            flops=6 * rows * width * TILE * tiles,
            bytes_accessed=4 * rows * width + 6 * (rows + width) * TILE * tiles,
            transcendentals=rows * TILE * tiles,
        ),
        name="hidden_units",
    )(act, cotan, weights, weights, weights, *waits)


def hidden_grad_kernel(act_ref, cot_ref, dgu_ref, inner_ref, out_ref):
    out_ref[:, : 2 * TILE] = dot(act_ref[...], dgu_ref[...]).astype(bf16)
    out_ref[:, 2 * TILE :] = dot(cot_ref[...], inner_ref[...]).astype(bf16)


def hidden_grad(act_turned, cot_turned, dgu, inner, *waits):
    width, rows = act_turned.shape
    tiles = inner.shape[1] // TILE
    whole = pl.BlockSpec((width, rows), lambda j: (0, 0))
    return pl.pallas_call(
        waiting(hidden_grad_kernel, 4, waits),
        grid=(tiles,),
        in_specs=[
            whole,
            whole,
            pl.BlockSpec((rows, 2 * TILE), lambda j: (0, j)),
            pl.BlockSpec((rows, TILE), lambda j: (0, j)),
        ]
        + [ANYWHERE] * len(waits),
        out_specs=pl.BlockSpec((width, 3 * TILE), lambda j: (0, j)),
        out_shape=jax.ShapeDtypeStruct((width, 3 * TILE * tiles), bf16),
        compiler_params=pltpu.CompilerParams(vmem_limit_bytes=VMEM),
        cost_estimate=pl.CostEstimate(
            flops=6 * rows * width * TILE * tiles,
            bytes_accessed=4 * rows * width + 6 * (rows + width) * TILE * tiles,
            transcendentals=0,
        ),
        name="hidden_grad",
    )(act_turned, cot_turned, dgu, inner, *waits)


def back_kernel(at, tall, values_ref, w_ref, *refs):
    made = None
    for t in range(values_ref.shape[1] // tall):
        start = 3 * TILE * t + at
        one = dot(values_ref[:, t * tall : (t + 1) * tall], w_ref[:, start : start + tall], ROWS)
        made = one if made is None else made + one
    for ref in refs[:-1]:
        made += ref[...]
    refs[-1][...] = made.astype(refs[-1].dtype)


def back(values, weights, at, tall, start, dtype, *waits):
    rows, columns = values.shape
    width = weights.shape[0]
    wide = 2 * TILE
    block = pl.BlockSpec((rows, wide), lambda j: (0, j))
    extra = [] if start is None else [start]
    return pl.pallas_call(
        waiting(functools.partial(back_kernel, at, tall), 2 + len(extra), waits),
        grid=(width // wide,),
        in_specs=[
            pl.BlockSpec((rows, columns), lambda j: (0, 0)),
            pl.BlockSpec((wide, weights.shape[1]), lambda j: (j, 0)),
        ]
        + [block] * len(extra)
        + [ANYWHERE] * len(waits),
        out_specs=block,
        out_shape=jax.ShapeDtypeStruct((rows, width), dtype),
        compiler_params=pltpu.CompilerParams(vmem_limit_bytes=VMEM),
        cost_estimate=pl.CostEstimate(
            flops=2 * rows * width * columns,
            bytes_accessed=2 * rows * (columns + 2 * width) + 2 * width * weights.shape[1],
            transcendentals=0,
        ),
        name="from_hidden",
    )(values, weights, *extra, *waits)


def adamw(weight, gradient, moment, square, step_size):
    moment_new = beta_one * moment + (1.0 - beta_one) * gradient
    square_new = beta_two * square + (1.0 - beta_two) * gradient * gradient
    moment_hat = moment_new / (1.0 - beta_one**STEP)
    square_hat = square_new / (1.0 - beta_two**STEP)
    weight_new = weight - step_size * (
        moment_hat / (jnp.sqrt(square_hat) + adam_eps) + decay_rate * weight
    )
    return (weight_new, moment_new, square_new)


def adam_kernel(step_size, g_ref, w_ref, m_ref, s_ref, go_ref, wo_ref, mo_ref, so_ref):
    gradient = g_ref[...].astype(f32)
    weight, moment, square = adamw(w_ref[0], gradient, m_ref[0], s_ref[0], step_size)
    go_ref[0] = gradient
    wo_ref[0] = weight
    mo_ref[0] = moment
    so_ref[0] = square


def adam(gradient, first, weight, moment, square, step_size, *waits):
    flat = weight.ndim == 2
    if flat:
        weight, moment, square = weight[None], moment[None], square[None]
    count, rows, columns = weight.shape
    tall = min(rows, max(16, 131072 // columns))
    block = pl.BlockSpec((1, tall, columns), lambda j, i: (j, i, 0))
    made = pl.pallas_call(
        waiting(functools.partial(adam_kernel, step_size), 4, waits),
        grid=(count, rows // tall),
        in_specs=[pl.BlockSpec((tall, columns), lambda j, i: (i, first + j)), block, block, block]
        + [ANYWHERE] * len(waits),
        out_specs=[block] * 4,
        out_shape=[jax.ShapeDtypeStruct(weight.shape, f32)] * 4,
        compiler_params=pltpu.CompilerParams(vmem_limit_bytes=VMEM),
        cost_estimate=pl.CostEstimate(
            flops=15 * weight.size, bytes_accessed=30 * weight.size, transcendentals=weight.size
        ),
        name="adamw",
    )(gradient, weight, moment, square, *waits)
    return [one[0] for one in made] if flat else made


def adam_hidden_kernel(steps, g_ref, *refs):
    gu, down, refs = refs[:3], refs[3:6], refs[6:]
    gu_out, down_out = refs[-8:-4], refs[-4:]
    gradient = g_ref[...].astype(f32)
    for n in range(2):
        own = gradient[:, n * TILE : (n + 1) * TILE]
        weight, moment, square = adamw(gu[0][n], own, gu[1][n], gu[2][n], steps[0])
        for ref, value in zip(gu_out, (own, weight, moment, square)):
            ref[n] = value
    own = gradient[:, 2 * TILE :]
    weight, moment, square = adamw(down[0][...], own, down[1][...], down[2][...], steps[1])
    for ref, value in zip(down_out, (own, weight, moment, square)):
        ref[...] = value


def adam_hidden(gradient, gateup, down, first, filled):
    rows = gradient.shape[0]
    tiles = gradient.shape[1] // (3 * TILE)
    two = pl.BlockSpec((2, rows, TILE), lambda j: (0, 0, first + j))
    one = pl.BlockSpec((rows, TILE), lambda j: (0, first + j))
    anywhere = pl.BlockSpec(memory_space=pl.ANY)
    filled = list(filled or [])
    return pl.pallas_call(
        functools.partial(adam_hidden_kernel, (0.4 / math.sqrt(D), 0.4 / math.sqrt(FF))),
        grid=(tiles,),
        in_specs=[pl.BlockSpec((rows, 3 * TILE), lambda j: (0, j))]
        + [two] * 3
        + [one] * 3
        + [anywhere] * len(filled),
        out_specs=[two] * 4 + [one] * 4,
        out_shape=[jax.ShapeDtypeStruct(gateup[0].shape, f32)] * 4
        + [jax.ShapeDtypeStruct(down[0].shape, f32)] * 4,
        input_output_aliases={7 + n: n for n in range(len(filled))},
        compiler_params=pltpu.CompilerParams(vmem_limit_bytes=VMEM),
        cost_estimate=pl.CostEstimate(
            flops=45 * rows * TILE * tiles,
            bytes_accessed=90 * rows * TILE * tiles,
            transcendentals=3 * rows * TILE * tiles,
        ),
        name="adamw_hidden",
    )(gradient, *gateup, *down, *filled)


def side_by_side(weight):
    return jnp.concatenate([weight[j].astype(bf16) for j in range(weight.shape[0])], 1)


def edges(rows, parts):
    return [rows * n // parts // 16 * 16 for n in range(parts)] + [rows]


def exchange(values, axis, bit):
    size = lax.axis_size(axis)
    return lax.ppermute(values, axis, [(i, i ^ bit) for i in range(size)])


def bits_of(axis):
    return [1 << n for n in range(lax.axis_size(axis).bit_length() - 1)]


def turns(bits):
    return [bits[n:] + bits[:n] for n in range(len(bits))]


def gather(own, arrived=None):
    bits = bits_of("tp")
    cut = edges(own.shape[0], len(bits))
    held = []
    for n, order in enumerate(turns(bits)):
        held.append(({0: own[cut[n] : cut[n + 1]]}, order))
    for step in range(len(bits)):
        for have, order in held:
            bit = order[step]
            got = {k ^ bit: exchange(v, "tp", bit) for k, v in list(have.items())}
            have.update(got)
            if arrived is not None:
                arrived.setdefault(step, []).extend(got.values())
    return [[have[k] for have, _ in held] for k in range(lax.axis_size("tp"))]


def scatter(partials, arrived=None):
    bits = bits_of("tp")
    cut = edges(partials[0].shape[0], len(bits))
    held = []
    for n, order in enumerate(turns(bits)):
        held.append((dict(enumerate(p[cut[n] : cut[n + 1]] for p in partials)), order))
    for step in range(len(bits)):
        for have, order in held:
            bit = order[step]
            for k in [k for k in have if k & bit]:
                got = exchange(have.pop(k).astype(bf16), "tp", bit)
                if arrived is not None:
                    arrived.setdefault(step, []).append(got)
                have[k ^ bit] = have[k ^ bit].astype(f32) + got.astype(f32)
    return jnp.concatenate([have[0] for have, _ in held], 0)


def to_partners(pieces):
    order = sorted(range(1, len(pieces)), key=lambda k: -bin(k).count("1"))
    got = {k: exchange(pieces[k], "tp", k) for k in order}
    return [pieces[0]] + [got[k] for k in range(1, len(pieces))]


def sum_everywhere(values):
    for axis in ("tp", "ctx", "fsdp"):
        for bit in bits_of(axis):
            values = values + exchange(values, axis, bit)
    return values


def residual_kernel(ranks, att_ref, x_ref, gain_ref, *refs):
    weights, (resid_ref, act_ref, scale_ref) = refs[:-3], refs[-3:]
    columns = att_ref.shape[1] // ranks
    parts = len(weights) // ranks
    made = []
    for n in range(parts):
        one = None
        for k in range(ranks):
            att = att_ref[:, k * columns : (k + 1) * columns]
            more = dot(att, weights[k * parts + n][...], ROWS)
            one = more if one is None else one + more
        made.append(one)
    resid = jnp.concatenate(made, 1) + x_ref[...].astype(f32)
    normed, scale = normalize(resid)
    resid_ref[...] = resid
    act_ref[...] = (normed * gain_ref[...]).astype(bf16)
    scale_ref[...] = scale


def residual(attended, tokens, gain, weights):
    rows, width = tokens.shape
    flat = [piece for pieces in weights for piece in pieces]
    return pl.pallas_call(
        functools.partial(residual_kernel, len(weights)),
        out_shape=[
            jax.ShapeDtypeStruct((rows, width), f32),
            jax.ShapeDtypeStruct((rows, width), bf16),
            jax.ShapeDtypeStruct((rows, 1), f32),
        ],
        compiler_params=pltpu.CompilerParams(vmem_limit_bytes=VMEM),
        cost_estimate=pl.CostEstimate(
            flops=2 * rows * width * width,
            bytes_accessed=2 * width * width + 12 * rows * width,
            transcendentals=0,
        ),
        name="residual",
    )(attended, tokens, gain, *flat)


def attended_back_kernel(ranks, d_ref, *refs):
    weights, outs = refs[:-ranks], refs[-ranks:]
    parts = len(weights) // ranks
    for k in range(ranks):
        one = None
        at = 0
        for n in range(parts):
            weight = weights[k * parts + n][...]
            more = dot(d_ref[:, at : at + weight.shape[0]], weight)
            at += weight.shape[0]
            one = more if one is None else one + more
        outs[k][...] = one.astype(bf16)


def attended_back(dresid, weights, *waits):
    rows, width = dresid.shape
    flat = [piece for pieces in weights for piece in pieces]
    return pl.pallas_call(
        waiting(functools.partial(attended_back_kernel, len(weights)), 1 + len(flat), waits),
        in_specs=[pl.BlockSpec(memory_space=pltpu.VMEM)] * (1 + len(flat)) + [ANYWHERE] * len(waits),
        out_shape=[jax.ShapeDtypeStruct((rows, one[0].shape[1]), bf16) for one in weights],
        compiler_params=pltpu.CompilerParams(vmem_limit_bytes=VMEM),
        cost_estimate=pl.CostEstimate(
            flops=2 * rows * width * width,
            bytes_accessed=2 * width * width + 4 * rows * width,
            transcendentals=0,
        ),
        name="attended_back",
    )(dresid, *flat, *waits)


def local(
    block_input,
    segment_ids,
    positions,
    out_cotangent,
    norm_gains,
    qkv_weight,
    outproj_weight,
    gateup_weight,
    down_weight,
    moment_norm,
    moment_qkv,
    moment_outproj,
    moment_gateup,
    moment_down,
    square_norm,
    square_qkv,
    square_outproj,
    square_gateup,
    square_down,
):
    seqs_here, tok_here, width = block_input.shape
    ranks = lax.axis_size("tp")
    assert seqs_here == 1 and tok_here % BLOCK == 0 and lax.axis_size("ctx") == 2
    assert all(lax.axis_size(axis) & (lax.axis_size(axis) - 1) == 0 for axis in ("tp", "fsdp"))
    rank = lax.axis_index("tp")
    half = lax.axis_index("ctx")
    rows_all = tok_here
    share = rows_all // ranks
    rows_axes = ("fsdp", "ctx")
    tiles = down_weight.shape[1] // TILE
    early = 5 * tiles // 8
    cuts = [(0, early), (early, tiles - early)]

    def part(values, k):
        return lax.dynamic_slice_in_dim(values, (rank ^ k) * share, share, 0)

    def mixed(values):
        return jnp.concatenate([part(values, k) for k in range(ranks)], 0)

    def natural(shares):
        first = shares[0][0]
        whole = jnp.zeros((rows_all,) + first.shape[1:], first.dtype)
        for k, pieces in enumerate(shares):
            at = (rank ^ k) * share
            for piece in pieces:
                whole = lax.dynamic_update_slice_in_dim(whole, piece, at, 0)
                at = at + piece.shape[0]
        return whole

    def flat(shares):
        return jnp.concatenate([piece for pieces in shares for piece in pieces], 0)

    def by_share(values):
        return [values[k * share : (k + 1) * share] for k in range(ranks)]

    attn16 = jnp.concatenate([side_by_side(qkv_weight), outproj_weight.astype(bf16)], 1)
    attn16 = lax.all_gather(attn16, rows_axes, axis=0, tiled=True)
    mlp16 = [
        lax.all_gather(
            pack(gateup_weight, down_weight, first, count), rows_axes, axis=0, tiled=True
        )
        for first, count in cuts
    ]
    gains16 = lax.all_gather(norm_gains.astype(bf16), rows_axes, axis=1, tiled=True)
    gain_attn = gains16[0].astype(f32)
    gain_mlp = gains16[1].astype(f32)
    columns = outproj_weight.shape[1]
    outproj_all = gather(attn16[:, 3 * columns :])

    seg_own = segment_ids.reshape(rows_all)
    seg_prev = lax.ppermute(seg_own, "ctx", [(0, 1)])
    seg_prev = jnp.where(half == 0, -1, seg_prev)
    seg_all = jnp.concatenate([seg_prev, seg_own])
    last_of_keys = seg_all.reshape(-1, BLOCK)[:, -1]
    first_of_queries = seg_own.reshape(-1, BLOCK)[:, 0]
    low = jnp.sum(
        (last_of_keys[None, :] < first_of_queries[:, None]).astype(jnp.int32), 1, dtype=jnp.int32
    )
    seg_col = seg_all[:, None]
    seg_row = seg_own[None, :]
    cosine, sine = rope_tables(positions.reshape(rows_all))

    tokens16 = block_input.reshape(rows_all, width)
    cotan16 = out_cotangent.reshape(rows_all, width)
    cotan_mixed = mixed(cotan16)
    cotan_turned = cotan_mixed.T
    normed_one, _ = normalize(tokens16.astype(f32))
    act_one = (normed_one * gain_attn).astype(bf16)
    query16, kv_own = project(act_one, attn16, 3 * columns, cosine, sine, cotan_turned)
    kv_prev = lax.ppermute(kv_own, "ctx", [(0, 1)])
    attended16, lse = attend(low, query16, kv_prev, kv_own, seg_col, seg_row)
    attended_own = jnp.concatenate(to_partners([part(attended16, k) for k in range(ranks)]), 1)
    own_tokens = part(tokens16, 0).astype(f32)
    resid, act_share, scale_two = residual(
        attended_own, part(tokens16, 0), gain_mlp[None], outproj_all
    )

    act_two = flat(gather(act_share))
    act_turned = act_two.T
    dact = made = None
    hidden_grads = []
    for n, weights in enumerate(mlp16):
        last = n == len(mlp16) - 1
        dtype = bf16 if last else f32
        dgu, inner = hidden(act_two, cotan_mixed, weights, *([] if made is None else [made]))
        if last:
            dact = back(dgu, weights, 0, 2 * TILE, dact, dtype)
            arrived = {}
            dact_two = scatter(by_share(dact), arrived)
            waits = [one for step in arrived.values() for one in step]
            local_grad = hidden_grad(act_turned, cotan_turned, dgu, inner, *waits)
        else:
            local_grad = hidden_grad(act_turned, cotan_turned, dgu, inner)
            dact = back(dgu, weights, 0, 2 * TILE, dact, dtype, local_grad)
            made = back(inner, weights, 2 * TILE, TILE, made, dtype, dact)
        hidden_grads.append(
            lax.psum_scatter(local_grad, rows_axes, scatter_dimension=0, tiled=True)
        )

    normed_two = resid * scale_two
    dnorm_two, gain_two = norm_back(dact_two, normed_two, scale_two, gain_mlp)
    dresid = part(cotan16, 0).astype(f32) + dnorm_two
    dresid16 = dresid.astype(bf16)

    pieces = attended_back(dresid16, outproj_all)
    made = back(inner, weights, 2 * TILE, TILE, made, dtype, pieces[0])
    pieces = to_partners(pieces)
    dattended16 = natural([[piece] for piece in pieces])
    dresid_mixed = flat(gather(dresid16))
    dquery16, dkv_prev, dkv_own = attend_back(
        low,
        query16,
        kv_prev,
        kv_own,
        seg_col,
        seg_row,
        lse,
        attended16,
        dattended16,
        cosine,
        sine,
        dresid_mixed,
        made,
    )
    gateup_state = (gateup_weight, moment_gateup, square_gateup)
    down_state = (down_weight, moment_down, square_down)
    filled = adam_hidden(hidden_grads[0], gateup_state, down_state, 0, None)
    dkv_got = lax.ppermute(dkv_prev, "ctx", [(1, 0)])
    outproj_local = dot(dresid_mixed, mixed(attended16), OVER).astype(bf16)
    dproj16 = join(dquery16, dkv_own, dkv_got, cosine, sine, outproj_local, filled[0])
    qkv_local = dot(act_one, dproj16, OVER).astype(bf16)
    attn_grad = lax.psum_scatter(
        jnp.concatenate([qkv_local, outproj_local], 1), rows_axes, scatter_dimension=0, tiled=True
    )
    out_share = resid + scatter(by_share(hold(made, dproj16)))
    dact_one = scatter(
        [dot(part(dproj16, k), attn16[:, : 3 * columns], ROWS).astype(bf16) for k in range(ranks)]
    )
    normed_own, scale_own = normalize(own_tokens)
    dnorm_one, gain_one = norm_back(dact_one, normed_own, scale_own, gain_attn)
    for (first, _), gradient in zip(cuts[1:], hidden_grads[1:]):
        filled = adam_hidden(gradient, gateup_state, down_state, first, filled)

    arrived = {}
    input_grad = natural(gather((dresid + dnorm_one).astype(bf16), arrived))
    block_out = natural(gather(hold(out_share.astype(bf16), filled[0], *arrived[0])))

    gateup_grad, new_gateup, new_moment_gateup, new_square_gateup = filled[:4]
    down_grad, new_down, new_moment_down, new_square_down = filled[4:]
    outproj_grad, new_outproj, new_moment_outproj, new_square_outproj = adam(
        attn_grad,
        3,
        outproj_weight,
        moment_outproj,
        square_outproj,
        0.4 / math.sqrt(D // 64),
        new_down,
    )
    qkv_grad, new_qkv, new_moment_qkv, new_square_qkv = adam(
        attn_grad, 0, qkv_weight, moment_qkv, square_qkv, 0.4 / math.sqrt(D), new_down
    )
    gains_all = sum_everywhere(hold(jnp.stack([gain_one, gain_two]), new_qkv, new_outproj))
    wide = norm_gains.shape[1]
    place = (lax.axis_index("fsdp") * lax.axis_size("ctx") + half) * wide
    norm_grad = lax.dynamic_slice_in_dim(gains_all, place, wide, 1)

    new_norm, new_moment_norm, new_square_norm = adamw(
        norm_gains, norm_grad, moment_norm, square_norm, 0.4
    )
    return (
        block_out.reshape(block_input.shape),
        input_grad.reshape(block_input.shape),
        norm_grad,
        qkv_grad,
        outproj_grad,
        gateup_grad,
        down_grad,
        new_norm,
        new_qkv,
        new_outproj,
        new_gateup,
        new_down,
        new_moment_norm,
        new_moment_qkv,
        new_moment_outproj,
        new_moment_gateup,
        new_moment_down,
        new_square_norm,
        new_square_qkv,
        new_square_outproj,
        new_square_gateup,
        new_square_down,
    )


def solution(mesh):
    tokens = P("fsdp", "ctx", None)
    ids = P("fsdp", "ctx")
    gains = P(None, ("fsdp", "ctx"))
    stacked = P(None, ("fsdp", "ctx"), "tp")
    single = P(("fsdp", "ctx"), "tp")
    parameters = (gains, stacked, single, stacked, single)
    return jax.shard_map(
        local,
        mesh=mesh,
        in_specs=(tokens, ids, ids, tokens) + parameters * 3,
        out_specs=(tokens, tokens) + parameters * 4,
        check_vma=False,
    )
```
